256 devices in a mesh: dp: 32 (over y, x, core), mp: 8 (over z).
Axes of the slice: x: 4, y: 4, z: 8, core: 2. Of those that a mesh axis runs over, the one named last changes fastest.
Arguments:
- tokens: bfloat16 [2048, 7168], P('dp', 'mp'), may hold values from -6 to 6
- expert_ids: int32 [2048, 8], P('dp'), may hold values from 0 to 31, all different within a row; in each aligned block of 64 rows (0 to 63, 64 to 127, ...) at most 24 rows name the same one
- route_weights: float32 [2048, 8], P('dp'), may hold values from 0.2 to 1
- placement_of: int32 [32], replicated, may hold values from 0 to 31, each once
- gate_weight: bfloat16 [32, 7168, 1024], P(None, 'dp', 'mp'), may hold values from -0.0625 to 0.0625
- up_weight: bfloat16 [32, 7168, 1024], P(None, 'dp', 'mp'), may hold values from -0.0625 to 0.0625
- down_weight: bfloat16 [32, 7168, 1024], P(None, 'dp', 'mp'), may hold values from -0.1875 to 0.1875
Outputs:
- rollout_gate: bfloat16 [32, 7168, 1024], P('dp', None, 'mp')
- rollout_up: bfloat16 [32, 7168, 1024], P('dp', None, 'mp')
- rollout_down: bfloat16 [32, 7168, 1024], P('dp', None, 'mp')
- rollout_scales: float32 [3, 32, 56, 8], P(None, 'dp', None, 'mp')
- mixed: bfloat16 [2048, 7168], P('dp', 'mp')
The draws below stay inside these ranges and needn't reach their ends.
Inputs may be any that keep to these rules, and one draw needn't show every extreme that they name: `expert_ids`: each row names 8 different experts. In each aligned block of 64 rows (the tokens of one index of dp) no expert is named by more than 24 rows, a bound that some block reaches. `placement_of`: A permutation; slot s is held by the owner of dp index s.
All inputs are finite; a program needn't handle non-finite values. Where the reference program divides by a largest or mean magnitude, that divisor is 1e-20 or more.
Results may differ from the reference program's by a relative error of at most 0.02.
Values may be sent and summed in bfloat16 or wider, within the bound.
A program may use at most 192 MiB of HBM per device.

```python
import math
import jax
import jax.numpy as jnp
import numpy as np
from jax import lax

D = 7168
FFW = 1024
EXP = 32
TOPK = 8
BLK = 128
TOK_DEV = 64
CAP = 24
TOKENS = 2048
N_DP = 32
N_MP = 8


def block_levels(own_key, extent, split, low, high):
    def one(dim, parts):
        draws = jax.random.uniform(jax.random.fold_in(jax.random.fold_in(own_key, 6), dim), (parts,), jnp.float32, low / len(split), high / len(split))
        return jnp.repeat(jnp.exp(draws), extent[dim] // parts).reshape((-1,) + (1,) * (len(extent) - dim - 1))

    factor_of = one(*split[0])
    for cut in split[1:]:
        factor_of = factor_of * one(*cut)
    return factor_of


def deal_out(own_key, own, number, rows, number_of, top, reach, lean):
    order = jax.random.permutation(own_key, number_of)
    packed, usual = portions_of(number_of, rows * top, reach, lean, True), portions_of(number_of, rows * top, reach, lean, False)
    places = jnp.arange(number_of)

    def named(tallies, turn):
        used = int((tallies > 0).sum())
        fixed = max(1, used // 4)
        shifted = fixed + (places - fixed + turn * (used - fixed)) % max(1, number_of - fixed)
        return jnp.zeros((number_of,), jnp.int32).at[order[jnp.where(places < fixed, places, shifted)]].set(jnp.asarray(tallies, jnp.int32))

    tallies = jnp.where(number % 4 == 0, named(packed, number // 4), named(usual, number - number // 4 - 1))
    mixed = jax.random.permutation(jax.random.fold_in(own, 3), number_of)
    donor, taker = mixed[0:number_of // 2 * 2:2], mixed[1:number_of // 2 * 2:2]
    margin = jnp.minimum(tallies[donor] - 1, reach - tallies[taker]) // 2
    margin = jnp.where((donor == order[0]) | (taker == order[0]) | (tallies[taker] == 0), 0, jnp.maximum(margin, 0))
    shifted = jax.random.randint(jax.random.fold_in(own, 4), (number_of // 2,), 0, 1 << 20) % (margin + 1)
    tallies = tallies.at[donor].add(-shifted).at[taker].add(shifted)
    labels = jnp.searchsorted(jnp.cumsum(tallies), jnp.arange(rows * top), side="right").astype(jnp.int32)
    table = labels.reshape(top, rows).T
    table = table[jax.random.permutation(jax.random.fold_in(own, 1), rows)]
    turn = jax.random.randint(jax.random.fold_in(own, 2), (rows, 1), 0, top)
    return jnp.take_along_axis(table, (jnp.arange(top)[None, :] + turn) % top, axis=1)


def portions_of(amount, total, bound, lean, full):
    portions = [(1 << 20) // math.isqrt(standing ** lean) + 1 for standing in range(1, amount + 1)]
    largest = bound if full else min(bound, max(-(-total // amount), total * portions[0] // sum(portions)))
    least = 1 if total - largest >= amount - 1 else 0
    given, surplus = [largest] + [least] * (amount - 1), total - largest - least * (amount - 1)
    while surplus > 0:
        movable = [i for i in range(1, amount) if given[i] < largest] or [i for i in range(1, amount) if given[i] < bound]
        pool, remaining = sum([portions[i] for i in movable]), surplus
        for i in movable:
            more = min(bound - given[i], max(1, remaining * portions[i] // pool), surplus)
            given[i] = given[i] + more
            surplus = surplus - more
    return np.array(given)


def scatter_about(stream_key, shape, width, most, split=(), held_as=jnp.bfloat16):
    drawn = width * jax.random.normal(stream_key, shape, jnp.float32)
    if split:
        drawn = drawn * block_levels(stream_key, shape, split, -0.22, 0.18)
    return jnp.clip(drawn, -most, most).astype(held_as)


def setup_inputs(seed: int = 0) -> dict:
    key_of = jax.random.split(jax.random.key(seed), 8)
    tokens = scatter_about(key_of[0], (TOKENS, D), 1.0, 6.0, ((0, 32), (1, 8)))
    expert_ids_keys = jax.random.split(jax.random.fold_in(key_of[1], 1), TOKENS // TOK_DEV)
    expert_ids_turns = jax.random.permutation(jax.random.fold_in(key_of[1], 3), TOKENS // TOK_DEV)
    expert_ids = jax.vmap(lambda own, number: deal_out(jax.random.fold_in(key_of[1], 2), own, number, TOK_DEV, EXP, TOPK, CAP, 1))(expert_ids_keys, expert_ids_turns).reshape((TOKENS, TOPK))
    route_weights = jnp.clip(0.2 + 0.8 * jax.random.uniform(key_of[2], (TOKENS, TOPK), jnp.float32) ** block_levels(key_of[2], (TOKENS, TOPK), ((0, 32),), -0.2, 0.2), 0.2, 1.0)
    placement_of = jax.random.permutation(key_of[3], EXP).astype(jnp.int32)
    gate_weight = scatter_about(key_of[4], (EXP, D, FFW), D ** -0.5, 0.0625, ((1, 32), (2, 8)))
    up_weight = scatter_about(key_of[5], (EXP, D, FFW), D ** -0.5, 0.0625, ((1, 32), (2, 8)))
    down_weight = scatter_about(key_of[6], (EXP, D, FFW), FFW ** -0.5, 0.1875, ((1, 32), (2, 8)))
    return {"tokens": tokens, "expert_ids": expert_ids, "route_weights": route_weights, "placement_of": placement_of, "gate_weight": gate_weight, "up_weight": up_weight, "down_weight": down_weight}


EPS = 1e-6


def quantize_block(matrix):
    rows, cols = matrix.shape
    blocks = matrix.astype(jnp.float32).reshape(rows // BLK, BLK, cols // BLK, BLK)
    scale = jnp.max(jnp.abs(blocks), axis=(1, 3)) + EPS
    quant = (blocks / scale[:, None, :, None]).astype(jnp.bfloat16).reshape(rows, cols)
    return quant, scale


def route_layout(expert_ids, route_weights, placement_of):
    flat = expert_ids.reshape(N_DP, TOK_DEV * TOPK)
    hits = (flat[:, :, None] == jnp.arange(EXP, dtype=jnp.int32)[None, None, :]).astype(jnp.int32)
    position = jnp.sum((jnp.cumsum(hits, axis=1) - hits) * hits, axis=2).astype(jnp.int32)
    owner_slot = jnp.take(placement_of, flat).astype(jnp.int32)
    sources = jnp.broadcast_to(jnp.arange(N_DP, dtype=jnp.int32)[:, None], flat.shape)
    token_index = jnp.broadcast_to(jnp.arange(TOKENS, dtype=jnp.int32).reshape(N_DP, TOK_DEV)[:, :, None], (N_DP, TOK_DEV, TOPK)).reshape(N_DP, -1)
    table = jnp.full((EXP, N_DP, CAP), TOKENS, jnp.int32).at[owner_slot, sources, position].set(token_index)
    weight_table = jnp.zeros((EXP, N_DP, CAP), jnp.float32).at[owner_slot, sources, position].set(route_weights.reshape(N_DP, -1).astype(jnp.float32))
    return table, weight_table


def expert_rows(rows, gate_q, gate_s, up_q, up_s, down_q, down_s):
    count = rows.shape[0]
    blocks_in = rows.astype(jnp.float32).reshape(count, D // BLK, BLK)

    def project(quant, scale):
        per_block = jnp.einsum("nkb,kbgf->nkgf", blocks_in, quant.astype(jnp.float32).reshape(D // BLK, BLK, FFW // BLK, BLK), precision=lax.Precision.HIGHEST)
        return jnp.einsum("nkgf,kg->ngf", per_block, scale, precision=lax.Precision.HIGHEST).reshape(count, FFW)

    gate = project(gate_q, gate_s)
    up = project(up_q, up_s)
    hidden = (jax.nn.silu(gate) * up).astype(jnp.bfloat16)
    hidden_blocks = hidden.astype(jnp.float32).reshape(count, FFW // BLK, BLK)
    per_block = jnp.einsum("ngf,kbgf->nkgb", hidden_blocks, down_q.astype(jnp.float32).reshape(D // BLK, BLK, FFW // BLK, BLK), precision=lax.Precision.HIGHEST)
    scaled = per_block * down_s[None, :, :, None]
    partial_value = jnp.sum(scaled.reshape(count, D // BLK, N_MP, FFW // BLK // N_MP, BLK), axis=3).astype(jnp.bfloat16)
    return jnp.sum(partial_value.astype(jnp.float32), axis=2).reshape(count, D)


def reference(tokens, expert_ids, route_weights, placement_of, gate_weight, up_weight, down_weight):
    inverse = jnp.argsort(placement_of).astype(jnp.int32)

    def quant_slot(index):
        expert = inverse[index]
        gate_q, gate_s = quantize_block(gate_weight[expert])
        up_q, up_s = quantize_block(up_weight[expert])
        down_q, down_s = quantize_block(down_weight[expert])
        return gate_q, gate_s, up_q, up_s, down_q, down_s

    gate_q, gate_s, up_q, up_s, down_q, down_s = lax.map(quant_slot, jnp.arange(EXP, dtype=jnp.int32))
    table, weight_table = route_layout(expert_ids, route_weights, placement_of)
    padded = jnp.concatenate([tokens, jnp.zeros((1, D), jnp.bfloat16)], axis=0)

    def one_slot(total, index):
        rows_index = table[index].reshape(-1)
        rows = padded[rows_index]
        result = expert_rows(rows, gate_q[index], gate_s[index], up_q[index], up_s[index], down_q[index], down_s[index])
        total = total.at[rows_index].add(weight_table[index].reshape(-1)[:, None] * result)
        return total, None

    total, _ = lax.scan(one_slot, jnp.zeros((TOKENS + 1, D), jnp.float32), jnp.arange(EXP, dtype=jnp.int32))
    mixed = total[:TOKENS].astype(jnp.bfloat16)
    scales = jnp.stack([gate_s, up_s, down_s])
    return gate_q, up_q, down_q, scales, mixed
```

```python
import jax
import jax.numpy as jnp
from jax import lax
from jax.experimental import pallas as pl
from jax.experimental.pallas import tpu as pltpu
from jax.sharding import PartitionSpec as P

BLK = 128
CAP = 24
EPS = 1e-06
NY, NX = 4, 4
NCH = 4
EARLY = 16
MESH = pl.DeviceIdType.MESH
F32, BF16 = jnp.float32, jnp.bfloat16


def routed_kernel(
    inv, ids4, rw4, tok, wg, wu, wd,
    fresh, mix,
    wog, wou, wod, wsg, wsu, wsd, packed, ids_all, pos_all, slot_w, tz, xs, xg, part,
    rg, ru, qg, qu, r2g, r2u, hid, outp, ob, zb,
    loc, ids_s, ids_r, z_s, z_r, t_s, t_r, w_s, w_r, r1_s, r1_r, r2_s, r2_r, a1_s, a2_s, a_r,
    o_s, o_r, zo_s, zo_r, f_s, f_r,
):
    dp, j = lax.axis_index("dp"), lax.axis_index("mp")
    n_dp, n_z = lax.axis_size("dp"), lax.axis_size("mp")
    nc = NX * NY
    c, h = dp // 2, dp % 2
    y, x = c // NX, c % NX
    sib = 2 * c + 1 - h
    n_e, dr, _ = wog.shape
    per = tz.shape[0] // n_z
    lanes = ids4.shape[1]
    tg = lanes // NX
    eb = n_e // NCH
    rows_ch = eb * CAP
    slots = n_e * CAP
    dc = 2 * dr

    def at(chip):
        return {"dp": 2 * chip + h, "mp": j}

    def remote(src, dst, ss, rs, dev):
        return pltpu.make_async_remote_copy(src_ref=src, dst_ref=dst, send_sem=ss, recv_sem=rs, device_id=dev, device_id_type=MESH)

    own_w = [pltpu.make_async_copy(a, b, loc.at[i]) for i, (a, b) in enumerate(((wg, wog), (wu, wou), (wd, wod)))]
    for cp in own_w:
        cp.start()
    own_tok = pltpu.make_async_copy(tok, tz.at[pl.ds(per * j, per)], loc.at[3])
    own_tok.start()

    lane_g = sum([(lax.broadcasted_iota(jnp.int32, (1, lanes), 1) >= i * tg).astype(jnp.int32) for i in range(1, NX)], jnp.zeros((1, lanes), jnp.int32))
    mine = jnp.where(lane_g == x, ids4[...], -1)
    ids_all[c] = mine

    barrier = pltpu.get_barrier_semaphore()

    def greet(k, _):
        pl.semaphore_signal(barrier, inc=1, device_id={"dp": (dp + k) % n_dp, "mp": j}, device_id_type=MESH)
        return 0

    lax.fori_loop(1, n_dp, greet, 0)

    def greet_z(k, _):
        pl.semaphore_signal(barrier, inc=1, device_id={"dp": dp, "mp": (j + k) % n_z}, device_id_type=MESH)
        return 0

    lax.fori_loop(1, n_z, greet_z, 0)
    pl.semaphore_wait(barrier, n_dp + n_z - 2)

    def z_copy(k):
        to = (j + k) % n_z
        return remote(tok, tz.at[pl.ds(per * j, per)], z_s.at[k], z_r.at[k], {"dp": dp, "mp": to})

    def z_start(k, _):
        z_copy(k).start()
        return 0

    lax.fori_loop(1, n_z, z_start, 0)

    def ids_copy(k):
        return remote(ids_all.at[c], ids_all.at[c], ids_s.at[k], ids_r.at[k], at((c + k) % nc))

    def ids_start(k, _):
        ids_copy(k).start()
        return 0

    lax.fori_loop(1, nc, ids_start, 0)
    sib_w = [
        remote(a, b, w_s.at[i], w_r.at[i], {"dp": sib, "mp": j})
        for i, (a, b) in enumerate(((wg, wsg), (wu, wsu), (wd, wsd)))
    ]
    for cp in sib_w:
        cp.start()

    for cp in own_w:
        cp.wait()

    def pack(s, _):
        e = inv[s]
        packed[s, 0] = wog[e]
        packed[s, 1] = wou[e]
        packed[s, 2] = wod[e]
        return 0

    lax.fori_loop(0, n_e, pack, 0)
    own_fresh = pltpu.make_async_copy(packed.at[dp], fresh.at[dp], loc.at[0])
    own_fresh.start()

    def f_copy(k):
        to = (dp + k) % n_dp
        return remote(packed.at[to], fresh.at[dp], f_s.at[k], f_r.at[k], {"dp": to, "mp": j})

    def f_start(k, _):
        f_copy(k).start()
        return 0

    early = min(EARLY, n_dp)
    lax.fori_loop(1, early, f_start, 0)

    lane_i = lax.broadcasted_iota(jnp.int32, (lanes, lanes), 1)
    row_i = lax.broadcasted_iota(jnp.int32, (lanes, lanes), 0)
    lane_of = sum([(lane_i >= i * tg).astype(jnp.int32) for i in range(1, NX)], jnp.zeros((lanes, lanes), jnp.int32))
    row_of = sum([(row_i >= i * tg).astype(jnp.int32) for i in range(1, NX)], jnp.zeros((lanes, lanes), jnp.int32))
    before = jnp.where((row_i < lane_i) & (lane_of == row_of), 1.0, 0.0).astype(BF16)
    e_iota = lax.broadcasted_iota(jnp.int32, (n_e, lanes), 0)
    top = ids4.shape[0]

    def positions(ids):
        named = jnp.zeros((n_e, lanes), F32)
        for i in range(top):
            named = jnp.where(ids[i : i + 1, :] == e_iota, 1.0, named)
        count = jnp.dot(named.astype(BF16), before, preferred_element_type=F32)
        return jnp.where(named > 0.5, count, -1.0)

    my_pos = positions(mine)
    my_w = jnp.zeros((n_e, lanes), F32)
    for i in range(top):
        my_w = jnp.where(mine[i : i + 1, :] == e_iota, rw4[i : i + 1, :], my_w)
    p_iota = lax.broadcasted_iota(jnp.int32, (CAP, lanes), 0).astype(F32)
    for q in range(NCH):
        pe = my_pos[q * eb : (q + 1) * eb, :].reshape(eb, 1, lanes)
        we = my_w[q * eb : (q + 1) * eb, :].reshape(eb, 1, lanes)
        ws = jnp.sum(jnp.where(pe == p_iota[None], we, 0.0), axis=2, keepdims=True)
        slot_w[q * rows_ch : (q + 1) * rows_ch, :] = jnp.broadcast_to(ws.reshape(rows_ch, 1), (rows_ch, BLK))

    own_tok.wait()

    def z_wait(k, _):
        src = (j + n_z - k) % n_z
        remote(tok, tz.at[pl.ds(per * src, per)], z_s.at[k], z_r.at[k], {"dp": dp, "mp": src}).wait_recv()
        return 0

    lax.fori_loop(1, n_z, z_wait, 0)

    def t_copy(k):
        to = (c + k) % nc
        return remote(tz.at[to], xs.at[c], t_s.at[k], t_r.at[k], at(to))

    def t_start(k, _):
        t_copy(k).start()
        return 0

    lax.fori_loop(1, nc, t_start, 0)
    own_x = pltpu.make_async_copy(tz.at[c], xs.at[c], loc.at[3])
    own_x.start()

    def ids_wait(k, _):
        src = (c + nc - k) % nc
        remote(ids_all.at[src], ids_all.at[src], ids_s.at[k], ids_r.at[k], at(src)).wait_recv()
        return 0

    lax.fori_loop(1, nc, ids_wait, 0)

    def place(b, _):
        ids = ids_all[b * NX]
        for i in range(1, NX):
            ids = jnp.maximum(ids, ids_all[b * NX + i])
        pos_all[b] = positions(ids)
        return 0

    lax.fori_loop(0, NY, place, 0)
    own_x.wait()

    def t_wait(k, _):
        src = (c + nc - k) % nc
        remote(tz.at[src], xs.at[src], t_s.at[k], t_r.at[k], at(src)).wait_recv()
        return 0

    lax.fori_loop(1, nc, t_wait, 0)
    for cp in sib_w:
        cp.wait_recv()

    r_iota = lax.broadcasted_iota(jnp.int32, (NX * CAP, lanes), 0)
    r_of = sum([(r_iota >= i * CAP).astype(jnp.int32) for i in range(1, NX)], jnp.zeros((NX * CAP, lanes), jnp.int32))
    want = jnp.where(r_of == lane_g, r_iota - CAP * r_of, -9).astype(F32)

    def one_hot(b, q):
        pe = pos_all[b, pl.ds(pl.multiple_of(q * eb, eb), eb), :].reshape(eb, 1, lanes)
        hot = jnp.where(pe == want[None], 1.0, 0.0).astype(BF16)
        return hot.reshape(eb * NX * CAP, lanes)

    def pick(q, b):
        tokens = xs[pl.ds(b * NX, NX)].reshape(lanes, dc)
        got = jnp.dot(one_hot(b, q), tokens, preferred_element_type=F32)
        xg[pl.ds(q * eb, eb), b] = got.astype(BF16).reshape(eb, NX * CAP, dc)

    def project(e):
        a = xg[e].reshape(NY * NX * CAP, dc)
        w = jnp.concatenate(
            [
                jnp.concatenate([wog[e], wou[e]], axis=1),
                jnp.concatenate([wsg[e], wsu[e]], axis=1),
            ],
            axis=0,
        )
        return jnp.dot(a, w, preferred_element_type=F32).reshape(nc, CAP, 2 * BLK)

    def rows_of(q):
        return pl.ds(pl.multiple_of(q * rows_ch, rows_ch), rows_ch)

    def r1_copy(q, k, up):
        if up:
            to = (y + k) % NY
            return remote(part.at[to, :, rows_of(q), pl.ds(BLK, BLK)], ru.at[k - 1, :, rows_of(q), :], r1_s.at[1, q, k - 1], r1_r.at[1, q, k - 1], at(to * NX + x))
        to = (x + k) % NX
        return remote(part.at[:, to, rows_of(q), pl.ds(0, BLK)], rg.at[k - 1, :, rows_of(q), :], r1_s.at[0, q, k - 1], r1_r.at[0, q, k - 1], at(y * NX + to))

    def first(q, _):
        for b in range(NY):
            pick(q, b)

        def pair(i, _):
            e = q * eb + 2 * i
            both = jnp.concatenate([project(e), project(e + 1)], axis=1).astype(BF16)
            part[:, :, pl.ds(pl.multiple_of(e * CAP, 2 * CAP), 2 * CAP), :] = both.reshape(NY, NX, 2 * CAP, 2 * BLK)
            return 0

        lax.fori_loop(0, eb // 2, pair, 0)
        for k in range(1, NX):
            r1_copy(q, k, False).start()
        for k in range(1, NY):
            r1_copy(q, k, True).start()
        return 0

    lax.fori_loop(0, NCH, first, 0)

    def r2_copy(q, k, up):
        if up:
            to = (x + k) % NX
            return remote(qu.at[to, rows_of(q), :], r2u.at[k - 1, rows_of(q), :], r2_s.at[1, q, k - 1], r2_r.at[1, q, k - 1], at(y * NX + to))
        to = (y + k) % NY
        return remote(qg.at[to, rows_of(q), :], r2g.at[k - 1, rows_of(q), :], r2_s.at[0, q, k - 1], r2_r.at[0, q, k - 1], at(to * NX + x))

    def second(q, _):
        rows = rows_of(q)
        for k in range(1, NX):
            r1_copy(q, k, False).wait_recv()

        def sum_g(i, _):
            t = part[i, x, rows, pl.ds(0, BLK)].astype(F32)
            for k in range(NX - 1):
                t = t + rg[k, i, rows, :].astype(F32)
            qg[i, rows, :] = t.astype(BF16)
            return 0

        lax.fori_loop(0, NY, sum_g, 0)
        for k in range(1, NY):
            r2_copy(q, k, False).start()
        for k in range(1, NY):
            r1_copy(q, k, True).wait_recv()

        def sum_u(i, _):
            t = part[y, i, rows, pl.ds(BLK, BLK)].astype(F32)
            for k in range(NY - 1):
                t = t + ru[k, i, rows, :].astype(F32)
            qu[i, rows, :] = t.astype(BF16)
            return 0

        lax.fori_loop(0, NX, sum_u, 0)
        for k in range(1, NX):
            r2_copy(q, k, True).start()
        return 0

    lax.fori_loop(0, NCH, second, 0)

    def line(q_along_x, k):
        if q_along_x:
            return y * NX + (x + k) % NX
        return ((y + k) % NY) * NX + x

    def a_copy(q, src, dev, ss):
        sl = hid.at[src // NX, src % NX, rows_of(q), :]
        return remote(sl, sl, ss, a_r.at[q, src], dev)

    def third(along_x):
        n1, n2 = (NX, NY) if along_x else (NY, NX)

        def body(q, _):
            rows = rows_of(q)
            for k in range(1, NY):
                r2_copy(q, k, False).wait_recv()
            for k in range(1, NX):
                r2_copy(q, k, True).wait_recv()
            gate = qg[y, rows, :].astype(F32)
            for k in range(NY - 1):
                gate = gate + r2g[k, rows, :].astype(F32)
            up = qu[x, rows, :].astype(F32)
            for k in range(NX - 1):
                up = up + r2u[k, rows, :].astype(F32)
            value = gate / (1.0 + jnp.exp(-gate)) * up * slot_w[rows, :]
            hid[y, x, rows, :] = value.astype(BF16)
            for k in range(1, n1):
                a_copy(q, c, at(line(along_x, k)), a1_s.at[q, k]).start()
            for k in range(1, n2):
                a_copy(q, c, at(line(not along_x, k)), a2_s.at[q, 0, k]).start()
            return 0

        return body

    half = NCH // 2
    lax.fori_loop(0, half, third(True), 0)
    lax.fori_loop(half, NCH, third(False), 0)

    def forward(along_x):
        n1, n2 = (NX, NY) if along_x else (NY, NX)

        def body(q, _):
            for k in range(1, n1):
                src = line(along_x, n1 - k)
                a_copy(q, src, at(src), a1_s.at[q, k]).wait_recv()
                for m in range(1, n2):
                    a_copy(q, src, at(line(not along_x, m)), a2_s.at[q, k, m]).start()
            return 0

        return body

    lax.fori_loop(0, half, forward(True), 0)
    lax.fori_loop(half, NCH, forward(False), 0)
    lax.fori_loop(early, n_dp, f_start, 0)

    def down(along_x):
        n1, n2 = (NX, NY) if along_x else (NY, NX)

        def body(q, _):
            for m in range(1, n2):
                for k in range(n1):
                    if along_x:
                        src = ((y + m) % NY) * NX + (x + k) % NX
                    else:
                        src = ((y + k) % NY) * NX + (x + m) % NX
                    a_copy(q, src, at(src), a1_s.at[q, 0]).wait_recv()

            def pair(i, _):
                e = q * eb + 2 * i
                both = hid[:, :, pl.ds(pl.multiple_of(e * CAP, 2 * CAP), 2 * CAP), :].astype(F32).reshape(nc, 2 * CAP, BLK)
                for o in range(2):
                    a = both[:, o * CAP : (o + 1) * CAP, :].reshape(nc * CAP, BLK).astype(BF16)
                    w = jnp.concatenate([wod[e + o], wsd[e + o]], axis=0)
                    got = lax.dot_general(a, w, (((1,), (1,)), ((), ())), preferred_element_type=F32)
                    xg[e + o] = got.astype(BF16).reshape(NY, NX * CAP, dc)
                return 0

            lax.fori_loop(0, eb // 2, pair, 0)
            return 0

        return body

    lax.fori_loop(0, half, down(True), 0)
    lax.fori_loop(half, NCH, down(False), 0)

    def o_copy(to):
        k = (to + nc - c) % nc
        return remote(outp.at[to], ob.at[c], o_s.at[k], o_r.at[k], at(to))

    def combine(b, _):
        total = jnp.zeros((lanes, dc), F32)
        for q in range(NCH):
            d = xg[pl.ds(q * eb, eb), b].reshape(eb * NX * CAP, dc)
            total = total + lax.dot_general(one_hot(b, q), d, (((0,), (0,)), ((), ())), preferred_element_type=F32)
        outp[pl.ds(b * NX, NX)] = total.astype(BF16).reshape(NX, tg, dc)
        for i in range(NX):
            to = b * NX + i

            @pl.when(to != c)
            def _():
                o_copy(to).start()

        return 0

    lax.fori_loop(0, NY, combine, 0)
    ob[c] = outp[c]

    def o_wait(k, _):
        src = (c + nc - k) % nc
        remote(outp.at[src], ob.at[src], o_s.at[k], o_r.at[k], at(src)).wait_recv()
        return 0

    lax.fori_loop(1, nc, o_wait, 0)

    def zo_copy(k):
        to = (j + k) % n_z
        return remote(ob.at[pl.ds(per * to, per)], zb.at[k], zo_s.at[k], zo_r.at[k], {"dp": dp, "mp": to})

    def zo_start(k, _):
        zo_copy(k).start()
        return 0

    lax.fori_loop(1, n_z, zo_start, 0)
    total = ob[pl.ds(per * j, per)].astype(F32)
    for k in range(1, n_z):
        zo_copy(k).wait_recv()
        total = total + zb[k].astype(F32)
    mix[...] = total.astype(BF16)

    own_fresh.wait()

    def f_wait(k, _):
        src = (dp + n_dp - k) % n_dp
        remote(packed.at[src], fresh.at[src], f_s.at[k], f_r.at[k], {"dp": src, "mp": j}).wait_recv()
        f_copy(k).wait_send()
        return 0

    lax.fori_loop(1, n_dp, f_wait, 0)

    def z_done(k, _):
        z_copy(k).wait_send()
        zo_copy(k).wait_send()
        return 0

    lax.fori_loop(1, n_z, z_done, 0)

    def plane_done(k, _):
        ids_copy(k).wait_send()
        t_copy(k).wait_send()
        o_copy((c + k) % nc).wait_send()
        return 0

    lax.fori_loop(1, nc, plane_done, 0)
    for cp in sib_w:
        cp.wait_send()

    def sums_done(q, _):
        for k in range(1, NX):
            r1_copy(q, k, False).wait_send()
            r2_copy(q, k, True).wait_send()
        for k in range(1, NY):
            r1_copy(q, k, True).wait_send()
            r2_copy(q, k, False).wait_send()
        return 0

    lax.fori_loop(0, NCH, sums_done, 0)

    def hid_done(along_x):
        n1, n2 = (NX, NY) if along_x else (NY, NX)

        def body(q, _):
            for k in range(1, n1):
                a_copy(q, c, at(c), a1_s.at[q, k]).wait_send()
            for k in range(n1):
                for m in range(1, n2):
                    a_copy(q, c, at(c), a2_s.at[q, k, m]).wait_send()
            return 0

        return body

    lax.fori_loop(0, half, hid_done(True), 0)
    lax.fori_loop(half, NCH, hid_done(False), 0)


def quantize_kernel(fresh, gate, up, down, scales):
    rows = gate.shape[1]
    for m, out in enumerate((gate, up, down)):
        w = fresh[:, m].reshape(rows // BLK, BLK, BLK).astype(F32)
        top = jnp.max(jnp.max(jnp.abs(w), axis=1, keepdims=True), axis=2, keepdims=True) + EPS
        out[0] = (w / top).astype(BF16).reshape(rows, BLK)
        scales[0, m] = jnp.broadcast_to(top, (rows // BLK, 1, BLK)).reshape(rows // BLK, BLK)


def local(tokens, expert_ids, route_weights, placement_of, gate_weight, up_weight, down_weight):
    n_dp, n_z = lax.axis_size("dp"), lax.axis_size("mp")
    nc = n_dp // 2
    n_e, dr, _ = gate_weight.shape
    tg, wide = tokens.shape
    top = expert_ids.shape[1]
    dc, per, lanes = 2 * dr, wide // (2 * dr), NX * tg
    slots = n_e * CAP
    h = lax.axis_index("dp") % 2

    order = jnp.arange(n_e, dtype=jnp.int32)
    inv = jnp.sum(jnp.where(placement_of[:, None] == order[None, :], order[:, None], 0), axis=0)
    pieces = tokens.reshape(tg, per, 2, dr)
    pieces = jnp.where(h == 0, pieces, pieces[:, :, ::-1]).reshape(tg, per, dc).transpose(1, 0, 2)
    ids4 = jnp.tile(expert_ids.T, (1, NX))
    rw4 = jnp.tile(route_weights.T, (1, NX))

    vm = pltpu.VMEM
    dma = pltpu.SemaphoreType.DMA
    hbm = pl.BlockSpec(memory_space=pl.ANY)
    vmem = pl.BlockSpec(memory_space=pltpu.VMEM)
    weights = [vm((n_e, dr, BLK), BF16)] * 6
    fresh, mix = pl.pallas_call(
        routed_kernel,
        out_shape=(
            jax.ShapeDtypeStruct((n_dp, 3, dr, BLK), BF16),
            jax.ShapeDtypeStruct((per, tg, dc), BF16),
        ),
        in_specs=[pl.BlockSpec(memory_space=pltpu.SMEM), vmem, vmem, vmem, hbm, hbm, hbm],
        out_specs=(hbm, vmem),
        scratch_shapes=weights
        + [
            vm((n_dp, 3, dr, BLK), BF16),
            vm((nc, top, lanes), jnp.int32),
            vm((NY, n_e, lanes), F32),
            vm((slots, BLK), F32),
            vm((nc, tg, dc), BF16),
            vm((nc, tg, dc), BF16),
            vm((n_e, NY, NX * CAP, dc), BF16),
            vm((NY, NX, slots, 2 * BLK), BF16),
            vm((NX - 1, NY, slots, BLK), BF16),
            vm((NY - 1, NX, slots, BLK), BF16),
            vm((NY, slots, BLK), BF16),
            vm((NX, slots, BLK), BF16),
            vm((NY - 1, slots, BLK), BF16),
            vm((NX - 1, slots, BLK), BF16),
            vm((NY, NX, slots, BLK), BF16),
            vm((nc, tg, dc), BF16),
            vm((nc, tg, dc), BF16),
            vm((n_z, per, tg, dc), BF16),
            dma((4,)),
            dma((nc,)), dma((nc,)),
            dma((n_z,)), dma((n_z,)),
            dma((nc,)), dma((nc,)),
            dma((3,)), dma((3,)),
            dma((2, NCH, 3)), dma((2, NCH, 3)),
            dma((2, NCH, 3)), dma((2, NCH, 3)),
            dma((NCH, 4)), dma((NCH, 4, 4)), dma((NCH, nc)),
            dma((nc,)), dma((nc,)),
            dma((n_z,)), dma((n_z,)),
            dma((n_dp,)), dma((n_dp,)),
        ],
        compiler_params=pltpu.CompilerParams(collective_id=0, has_side_effects=True, vmem_limit_bytes=62 * 1024 * 1024),
    )(inv, ids4, rw4, pieces, gate_weight, up_weight, down_weight)

    step = max(1, BLK // dr if dr < BLK else 4)
    rows = step * dr
    grid = n_dp // step
    out_w = jax.ShapeDtypeStruct((1, n_dp * dr, BLK), BF16)
    spec_w = pl.BlockSpec((1, rows, BLK), lambda i: (0, i, 0))
    gate_q, up_q, down_q, scales = pl.pallas_call(
        quantize_kernel,
        grid=(grid,),
        out_shape=(out_w, out_w, out_w, jax.ShapeDtypeStruct((grid, 3, rows // BLK, BLK), F32)),
        in_specs=[pl.BlockSpec((step, 3, dr, BLK), lambda i: (i, 0, 0, 0))],
        out_specs=(spec_w, spec_w, spec_w, pl.BlockSpec((1, 3, rows // BLK, BLK), lambda i: (i, 0, 0, 0))),
    )(fresh)
    scales = scales[:, :, :, 0].transpose(1, 0, 2).reshape(3, 1, -1, 1)

    mixed = mix.transpose(1, 0, 2).reshape(tg, per, 2, dr)
    mixed = jnp.where(h == 0, mixed, mixed[:, :, ::-1]).reshape(tg, wide)
    return gate_q, up_q, down_q, scales, mixed


def solution(mesh):
    placed = (
        P("dp", "mp"),
        P("dp", None),
        P("dp", None),
        P(),
        P(None, "dp", "mp"),
        P(None, "dp", "mp"),
        P(None, "dp", "mp"),
    )
    return jax.shard_map(
        local,
        mesh=mesh,
        in_specs=placed,
        out_specs=(
            P("dp", None, "mp"),
            P("dp", None, "mp"),
            P("dp", None, "mp"),
            P(None, "dp", None, "mp"),
            P("dp", "mp"),
        ),
        check_vma=False,
    )
```

```python
import jax
import jax.numpy as jnp
from jax import lax
from jax.experimental import pallas as pl
from jax.experimental.pallas import tpu as pltpu
from jax.sharding import PartitionSpec as P

BLK = 128
CAP = 24
EPS = 1e-06
NY, NX = 4, 4
NCH = 4
EARLY = 1
MESH = pl.DeviceIdType.MESH
F32, BF16 = jnp.float32, jnp.bfloat16


def routed_kernel(
    inv, ids, rw, tok, wg, wu, wd,
    fresh, mix,
    wog, wou, wod, wsg, wsu, wsd, packed, st_a, st_b, tokp, ids_all, pos_all, slot_w, tz, xs, xg, part,
    rg, ru, qg, qu, r2g, r2u, hid, outp, ob, zb,
    loc, ids_s, ids_r, z_s, z_r, t_s, t_r, w_s, w_r, r1_s, r1_r, r2_s, r2_r, a1_s, a2_s, a_r,
    o_s, o_r, zo_s, zo_r, f1_s, f1_r, f2_s, f2_r,
):
    dp, j = lax.axis_index("dp"), lax.axis_index("mp")
    n_dp, n_z = lax.axis_size("dp"), lax.axis_size("mp")
    nc = NX * NY
    c, h = dp // 2, dp % 2
    y, x = c // NX, c % NX
    sib = 2 * c + 1 - h
    n_e, dr, _ = wog.shape
    per = tz.shape[0] // n_z
    top, tg = ids.shape
    lanes = NX * tg
    eb = n_e // NCH
    rows_ch = eb * CAP
    slots = n_e * CAP
    dc = 2 * dr

    def at(chip):
        return {"dp": 2 * chip + h, "mp": j}

    def remote(src, dst, ss, rs, dev):
        return pltpu.make_async_remote_copy(src_ref=src, dst_ref=dst, send_sem=ss, recv_sem=rs, device_id=dev, device_id_type=MESH)

    own_w = [pltpu.make_async_copy(a, b, loc.at[i]) for i, (a, b) in enumerate(((wg, wog), (wu, wou), (wd, wod)))]
    for cp in own_w:
        cp.start()
    for i in range(per):
        tokp[i] = tok[:, i * dc : (i + 1) * dc]
    own_tok = pltpu.make_async_copy(tokp, tz.at[pl.ds(per * j, per)], loc.at[3])
    own_tok.start()

    lane_g = sum([(lax.broadcasted_iota(jnp.int32, (1, lanes), 1) >= i * tg).astype(jnp.int32) for i in range(1, NX)], jnp.zeros((1, lanes), jnp.int32))
    mine = jnp.where(lane_g == x, jnp.concatenate([ids[...]] * NX, axis=1), -1)
    ids_all[c] = mine

    barrier = pltpu.get_barrier_semaphore()

    def greet(k, _):
        pl.semaphore_signal(barrier, inc=1, device_id={"dp": (dp + k) % n_dp, "mp": j}, device_id_type=MESH)
        return 0

    lax.fori_loop(1, n_dp, greet, 0)

    def greet_z(k, _):
        pl.semaphore_signal(barrier, inc=1, device_id={"dp": dp, "mp": (j + k) % n_z}, device_id_type=MESH)
        return 0

    lax.fori_loop(1, n_z, greet_z, 0)
    pl.semaphore_wait(barrier, n_dp + n_z - 2)

    def z_copy(k):
        to = (j + k) % n_z
        return remote(tokp, tz.at[pl.ds(per * j, per)], z_s.at[k], z_r.at[k], {"dp": dp, "mp": to})

    def z_start(k, _):
        z_copy(k).start()
        return 0

    lax.fori_loop(1, n_z, z_start, 0)

    def ids_copy(k):
        return remote(ids_all.at[c], ids_all.at[c], ids_s.at[k], ids_r.at[k], at((c + k) % nc))

    def ids_start(k, _):
        ids_copy(k).start()
        return 0

    lax.fori_loop(1, nc, ids_start, 0)
    sib_w = [
        remote(a, b, w_s.at[i], w_r.at[i], {"dp": sib, "mp": j})
        for i, (a, b) in enumerate(((wg, wsg), (wu, wsu), (wd, wsd)))
    ]
    for cp in sib_w:
        cp.start()

    for cp in own_w:
        cp.wait()

    def pack(s, _):
        e = inv[s]
        to = (s // (2 * NX), (s // 2) % NX, s % 2)
        packed[to[0], to[1], to[2], 0] = wog[e]
        packed[to[0], to[1], to[2], 1] = wou[e]
        packed[to[0], to[1], to[2], 2] = wod[e]
        return 0

    lax.fori_loop(0, n_e, pack, 0)
    hr = dr // 2
    top_rows, low_rows = pl.ds(0, hr), pl.ds(hr, hr)

    def f1_copy(k, low):
        if low:
            to = (y + k) % NY
            return remote(packed.at[to, :, :, :, low_rows, :], st_b.at[y], f1_s.at[1, k - 1], f1_r.at[1, k - 1], at(to * NX + x))
        to = (x + k) % NX
        return remote(packed.at[:, to, :, :, top_rows, :], st_a.at[x], f1_s.at[0, k - 1], f1_r.at[0, k - 1], at(y * NX + to))

    def f1_from(k, low):
        if low:
            src = (y + NY - k) % NY
            return remote(packed.at[y, :, :, :, low_rows, :], st_b.at[src], f1_s.at[1, k - 1], f1_r.at[1, k - 1], at(src * NX + x))
        src = (x + NX - k) % NX
        return remote(packed.at[:, x, :, :, top_rows, :], st_a.at[src], f1_s.at[0, k - 1], f1_r.at[0, k - 1], at(y * NX + src))

    f1_own = [
        pltpu.make_async_copy(packed.at[:, x, :, :, top_rows, :], st_a.at[x], loc.at[4]),
        pltpu.make_async_copy(packed.at[y, :, :, :, low_rows, :], st_b.at[y], loc.at[5]),
    ]

    def f2_copy(k, d, low):
        core = (h + d) % 2
        if low:
            to = (x + k) % NX
            return remote(st_b.at[:, to, core], fresh.at[:, x, h, :, low_rows, :], f2_s.at[1, k, d], f2_r.at[1, k, d], {"dp": 2 * (y * NX + to) + core, "mp": j})
        to = (y + k) % NY
        return remote(st_a.at[:, to, core], fresh.at[y, :, h, :, top_rows, :], f2_s.at[0, k, d], f2_r.at[0, k, d], {"dp": 2 * (to * NX + x) + core, "mp": j})

    def f2_from(k, d, low):
        core = (h + d) % 2
        if low:
            src = (x + NX - k) % NX
            return remote(st_b.at[:, x, h], fresh.at[:, src, core, :, low_rows, :], f2_s.at[1, k, d], f2_r.at[1, k, d], {"dp": 2 * (y * NX + src) + core, "mp": j})
        src = (y + NY - k) % NY
        return remote(st_a.at[:, y, h], fresh.at[src, :, core, :, top_rows, :], f2_s.at[0, k, d], f2_r.at[0, k, d], {"dp": 2 * (src * NX + x) + core, "mp": j})

    f2_own = [
        pltpu.make_async_copy(st_a.at[:, y, h], fresh.at[y, :, h, :, top_rows, :], loc.at[4]),
        pltpu.make_async_copy(st_b.at[:, x, h], fresh.at[:, x, h, :, low_rows, :], loc.at[5]),
    ]
    steps = [(k, d) for k in range(max(NX, NY)) for d in range(2) if k or d]

    def f2_start(ks):
        for k, d in steps:
            if k in ks:
                if k < NY:
                    f2_copy(k, d, False).start()
                if k < NX:
                    f2_copy(k, d, True).start()

    for cp in f1_own:
        cp.start()
    for k in range(1, NX):
        f1_copy(k, False).start()
    for k in range(1, NY):
        f1_copy(k, True).start()

    lane_i = lax.broadcasted_iota(jnp.int32, (lanes, lanes), 1)
    row_i = lax.broadcasted_iota(jnp.int32, (lanes, lanes), 0)
    lane_of = sum([(lane_i >= i * tg).astype(jnp.int32) for i in range(1, NX)], jnp.zeros((lanes, lanes), jnp.int32))
    row_of = sum([(row_i >= i * tg).astype(jnp.int32) for i in range(1, NX)], jnp.zeros((lanes, lanes), jnp.int32))
    before = jnp.where((row_i < lane_i) & (lane_of == row_of), 1.0, 0.0).astype(BF16)
    e_iota = lax.broadcasted_iota(jnp.int32, (n_e, lanes), 0)
    rw4 = jnp.concatenate([rw[...]] * NX, axis=1)

    def positions(ids):
        named = jnp.zeros((n_e, lanes), F32)
        for i in range(top):
            named = jnp.where(ids[i : i + 1, :] == e_iota, 1.0, named)
        count = jnp.dot(named.astype(BF16), before, preferred_element_type=F32)
        return jnp.where(named > 0.5, count, -1.0)

    my_pos = positions(mine)
    my_w = jnp.zeros((n_e, lanes), F32)
    for i in range(top):
        my_w = jnp.where(mine[i : i + 1, :] == e_iota, rw4[i : i + 1, :], my_w)
    p_iota = lax.broadcasted_iota(jnp.int32, (CAP, lanes), 0).astype(F32)
    for q in range(NCH):
        pe = my_pos[q * eb : (q + 1) * eb, :].reshape(eb, 1, lanes)
        we = my_w[q * eb : (q + 1) * eb, :].reshape(eb, 1, lanes)
        ws = jnp.sum(jnp.where(pe == p_iota[None], we, 0.0), axis=2, keepdims=True)
        slot_w[q * rows_ch : (q + 1) * rows_ch, :] = jnp.broadcast_to(ws.reshape(rows_ch, 1), (rows_ch, BLK))

    own_tok.wait()

    def z_wait(k, _):
        src = (j + n_z - k) % n_z
        remote(tokp, tz.at[pl.ds(per * src, per)], z_s.at[k], z_r.at[k], {"dp": dp, "mp": src}).wait_recv()
        return 0

    lax.fori_loop(1, n_z, z_wait, 0)

    def t_copy(k):
        to = (c + k) % nc
        return remote(tz.at[to], xs.at[c], t_s.at[k], t_r.at[k], at(to))

    def t_start(k, _):
        t_copy(k).start()
        return 0

    lax.fori_loop(1, nc, t_start, 0)
    own_x = pltpu.make_async_copy(tz.at[c], xs.at[c], loc.at[3])
    own_x.start()

    def ids_wait(k, _):
        src = (c + nc - k) % nc
        remote(ids_all.at[src], ids_all.at[src], ids_s.at[k], ids_r.at[k], at(src)).wait_recv()
        return 0

    lax.fori_loop(1, nc, ids_wait, 0)

    def place(b, _):
        ids = ids_all[b * NX]
        for i in range(1, NX):
            ids = jnp.maximum(ids, ids_all[b * NX + i])
        pos_all[b] = positions(ids)
        return 0

    lax.fori_loop(0, NY, place, 0)
    own_x.wait()

    def t_wait(k, _):
        src = (c + nc - k) % nc
        remote(tz.at[src], xs.at[src], t_s.at[k], t_r.at[k], at(src)).wait_recv()
        return 0

    lax.fori_loop(1, nc, t_wait, 0)
    for cp in sib_w:
        cp.wait_recv()

    for cp in f1_own:
        cp.wait()
    for k in range(1, NX):
        f1_from(k, False).wait_recv()
    for k in range(1, NY):
        f1_from(k, True).wait_recv()
    for cp in f2_own:
        cp.start()
    f2_start(range(EARLY))

    r_iota = lax.broadcasted_iota(jnp.int32, (NX * CAP, lanes), 0)
    r_of = sum([(r_iota >= i * CAP).astype(jnp.int32) for i in range(1, NX)], jnp.zeros((NX * CAP, lanes), jnp.int32))
    want = jnp.where(r_of == lane_g, r_iota - CAP * r_of, -9).astype(F32)

    def one_hot(b, q):
        pe = pos_all[b, pl.ds(pl.multiple_of(q * eb, eb), eb), :].reshape(eb, 1, lanes)
        hot = jnp.where(pe == want[None], 1.0, 0.0).astype(BF16)
        return hot.reshape(eb * NX * CAP, lanes)

    def pick(q, b):
        tokens = xs[pl.ds(b * NX, NX)].reshape(lanes, dc)
        got = jnp.dot(one_hot(b, q), tokens, preferred_element_type=F32)
        xg[pl.ds(q * eb, eb), b] = got.astype(BF16).reshape(eb, NX * CAP, dc)

    def by_core(own, other):
        return jnp.concatenate([jnp.where(h == 0, own, other), jnp.where(h == 0, other, own)], axis=0)

    def project(e):
        a = xg[e].reshape(NY * NX * CAP, dc)
        w = jnp.concatenate([by_core(wog[e], wsg[e]), by_core(wou[e], wsu[e])], axis=1)
        return jnp.dot(a, w, preferred_element_type=F32).reshape(nc, CAP, 2 * BLK)

    def rows_of(q):
        return pl.ds(pl.multiple_of(q * rows_ch, rows_ch), rows_ch)

    def r1_copy(q, k, up):
        if up:
            to = (y + k) % NY
            return remote(part.at[to, :, rows_of(q), pl.ds(BLK, BLK)], ru.at[k - 1, :, rows_of(q), :], r1_s.at[1, q, k - 1], r1_r.at[1, q, k - 1], at(to * NX + x))
        to = (x + k) % NX
        return remote(part.at[:, to, rows_of(q), pl.ds(0, BLK)], rg.at[k - 1, :, rows_of(q), :], r1_s.at[0, q, k - 1], r1_r.at[0, q, k - 1], at(y * NX + to))

    def first(q, _):
        for b in range(NY):
            pick(q, b)

        def pair(i, _):
            e = q * eb + 2 * i
            both = jnp.concatenate([project(e), project(e + 1)], axis=1).astype(BF16)
            part[:, :, pl.ds(pl.multiple_of(e * CAP, 2 * CAP), 2 * CAP), :] = both.reshape(NY, NX, 2 * CAP, 2 * BLK)
            return 0

        lax.fori_loop(0, eb // 2, pair, 0)
        for k in range(1, NX):
            r1_copy(q, k, False).start()
        for k in range(1, NY):
            r1_copy(q, k, True).start()
        return 0

    lax.fori_loop(0, NCH, first, 0)

    def r2_copy(q, k, up):
        if up:
            to = (x + k) % NX
            return remote(qu.at[to, rows_of(q), :], r2u.at[k - 1, rows_of(q), :], r2_s.at[1, q, k - 1], r2_r.at[1, q, k - 1], at(y * NX + to))
        to = (y + k) % NY
        return remote(qg.at[to, rows_of(q), :], r2g.at[k - 1, rows_of(q), :], r2_s.at[0, q, k - 1], r2_r.at[0, q, k - 1], at(to * NX + x))

    def second(q, _):
        rows = rows_of(q)
        for k in range(1, NX):
            r1_copy(q, k, False).wait_recv()

        def sum_g(i, _):
            t = part[i, x, rows, pl.ds(0, BLK)].astype(F32)
            for k in range(NX - 1):
                t = t + rg[k, i, rows, :].astype(F32)
            qg[i, rows, :] = t.astype(BF16)
            return 0

        lax.fori_loop(0, NY, sum_g, 0)
        for k in range(1, NY):
            r2_copy(q, k, False).start()
        for k in range(1, NY):
            r1_copy(q, k, True).wait_recv()

        def sum_u(i, _):
            t = part[y, i, rows, pl.ds(BLK, BLK)].astype(F32)
            for k in range(NY - 1):
                t = t + ru[k, i, rows, :].astype(F32)
            qu[i, rows, :] = t.astype(BF16)
            return 0

        lax.fori_loop(0, NX, sum_u, 0)
        for k in range(1, NX):
            r2_copy(q, k, True).start()
        return 0

    lax.fori_loop(0, NCH, second, 0)

    def line(q_along_x, k):
        if q_along_x:
            return y * NX + (x + k) % NX
        return ((y + k) % NY) * NX + x

    def a_copy(q, src, dev, ss):
        sl = hid.at[src // NX, src % NX, rows_of(q), :]
        return remote(sl, sl, ss, a_r.at[q, src], dev)

    def third(along_x):
        n1, n2 = (NX, NY) if along_x else (NY, NX)

        def body(q, _):
            rows = rows_of(q)
            for k in range(1, NY):
                r2_copy(q, k, False).wait_recv()
            for k in range(1, NX):
                r2_copy(q, k, True).wait_recv()
            gate = qg[y, rows, :].astype(F32)
            for k in range(NY - 1):
                gate = gate + r2g[k, rows, :].astype(F32)
            up = qu[x, rows, :].astype(F32)
            for k in range(NX - 1):
                up = up + r2u[k, rows, :].astype(F32)
            value = gate / (1.0 + jnp.exp(-gate)) * up * slot_w[rows, :]
            hid[y, x, rows, :] = value.astype(BF16)
            for k in range(1, n1):
                a_copy(q, c, at(line(along_x, k)), a1_s.at[q, k]).start()
            for k in range(1, n2):
                a_copy(q, c, at(line(not along_x, k)), a2_s.at[q, 0, k]).start()
            return 0

        return body

    half = NCH // 2
    lax.fori_loop(0, half, third(True), 0)
    lax.fori_loop(half, NCH, third(False), 0)

    def forward(along_x):
        n1, n2 = (NX, NY) if along_x else (NY, NX)

        def body(q, _):
            for k in range(1, n1):
                src = line(along_x, n1 - k)
                a_copy(q, src, at(src), a1_s.at[q, k]).wait_recv()
                for m in range(1, n2):
                    a_copy(q, src, at(line(not along_x, m)), a2_s.at[q, k, m]).start()
            return 0

        return body

    lax.fori_loop(0, half, forward(True), 0)
    lax.fori_loop(half, NCH, forward(False), 0)
    f2_start(range(EARLY, max(NX, NY)))

    def down(along_x):
        n1, n2 = (NX, NY) if along_x else (NY, NX)

        def body(q, _):
            for m in range(1, n2):
                for k in range(n1):
                    if along_x:
                        src = ((y + m) % NY) * NX + (x + k) % NX
                    else:
                        src = ((y + k) % NY) * NX + (x + m) % NX
                    a_copy(q, src, at(src), a1_s.at[q, 0]).wait_recv()

            def pair(i, _):
                e = q * eb + 2 * i
                both = hid[:, :, pl.ds(pl.multiple_of(e * CAP, 2 * CAP), 2 * CAP), :].astype(F32).reshape(nc, 2 * CAP, BLK)
                for o in range(2):
                    a = both[:, o * CAP : (o + 1) * CAP, :].reshape(nc * CAP, BLK).astype(BF16)
                    w = by_core(wod[e + o], wsd[e + o])
                    got = lax.dot_general(a, w, (((1,), (1,)), ((), ())), preferred_element_type=F32)
                    xg[e + o] = got.astype(BF16).reshape(NY, NX * CAP, dc)
                return 0

            lax.fori_loop(0, eb // 2, pair, 0)
            return 0

        return body

    lax.fori_loop(0, half, down(True), 0)
    lax.fori_loop(half, NCH, down(False), 0)

    def o_copy(to):
        k = (to + nc - c) % nc
        return remote(outp.at[to], ob.at[c], o_s.at[k], o_r.at[k], at(to))

    def zo_copy(to):
        k = (to + n_z - j) % n_z
        return remote(ob.at[pl.ds(per * to, per)], zb.at[k], zo_s.at[k], zo_r.at[k], {"dp": dp, "mp": to})

    def from_z(k):
        src = (j + n_z - k) % n_z
        return remote(ob.at[pl.ds(per * src, per)], zb.at[k], zo_s.at[k], zo_r.at[k], {"dp": dp, "mp": src})

    def combine(i, _):
        b = (y + 1 + i) % NY
        total = jnp.zeros((lanes, dc), F32)
        for q in range(NCH):
            d = xg[pl.ds(q * eb, eb), b].reshape(eb * NX * CAP, dc)
            total = total + lax.dot_general(one_hot(b, q), d, (((0,), (0,)), ((), ())), preferred_element_type=F32)
        outp[pl.ds(b * NX, NX)] = total.astype(BF16).reshape(NX, tg, dc)
        for n in range(NX):
            to = b * NX + n

            @pl.when(to != c)
            def _():
                o_copy(to).start()

        return 0

    def on_to_planes(i):
        row = (y + 2 * NY - 1 - i) % NY
        for n in range(NX):
            src = row * NX + n

            @pl.when(src != c)
            def _():
                k = (c + nc - src) % nc
                remote(outp.at[src], ob.at[src], o_s.at[k], o_r.at[k], at(src)).wait_recv()

        for n in range(NX // per):
            to = row * (NX // per) + n

            @pl.when(to != j)
            def _():
                zo_copy(to).start()

    def rows_step(i, _):
        combine(i, 0)

        @pl.when(i > 0)
        def _():
            on_to_planes(i - 1)

        return 0

    lax.fori_loop(0, NY, rows_step, 0)
    ob[c] = outp[c]
    on_to_planes(NY - 1)
    total = ob[pl.ds(per * j, per)].astype(F32)
    for k in range(1, n_z):
        from_z(k).wait_recv()
        total = total + zb[k].astype(F32)
    mix[...] = jnp.concatenate([total[i] for i in range(per)], axis=1).astype(BF16)

    for cp in f2_own:
        cp.wait()
    for k, d in steps:
        if k < NY:
            f2_from(k, d, False).wait_recv()
            f2_copy(k, d, False).wait_send()
        if k < NX:
            f2_from(k, d, True).wait_recv()
            f2_copy(k, d, True).wait_send()
    for k in range(1, NX):
        f1_copy(k, False).wait_send()
    for k in range(1, NY):
        f1_copy(k, True).wait_send()
    def z_done(k, _):
        z_copy(k).wait_send()
        zo_copy((j + k) % n_z).wait_send()
        return 0

    lax.fori_loop(1, n_z, z_done, 0)

    def plane_done(k, _):
        ids_copy(k).wait_send()
        t_copy(k).wait_send()
        o_copy((c + k) % nc).wait_send()
        return 0

    lax.fori_loop(1, nc, plane_done, 0)
    for cp in sib_w:
        cp.wait_send()

    def sums_done(q, _):
        for k in range(1, NX):
            r1_copy(q, k, False).wait_send()
            r2_copy(q, k, True).wait_send()
        for k in range(1, NY):
            r1_copy(q, k, True).wait_send()
            r2_copy(q, k, False).wait_send()
        return 0

    lax.fori_loop(0, NCH, sums_done, 0)

    def hid_done(along_x):
        n1, n2 = (NX, NY) if along_x else (NY, NX)

        def body(q, _):
            for k in range(1, n1):
                a_copy(q, c, at(c), a1_s.at[q, k]).wait_send()
            for k in range(n1):
                for m in range(1, n2):
                    a_copy(q, c, at(c), a2_s.at[q, k, m]).wait_send()
            return 0

        return body

    lax.fori_loop(0, half, hid_done(True), 0)
    lax.fori_loop(half, NCH, hid_done(False), 0)


def quantize_kernel(fresh, gate, up, down, scales):
    rows = gate.shape[1]
    for m, out in enumerate((gate, up, down)):
        w = fresh[:, m].reshape(rows // BLK, BLK, BLK).astype(F32)
        top = jnp.max(jnp.max(jnp.abs(w), axis=1, keepdims=True), axis=2, keepdims=True) + EPS
        out[0] = (w * (1.0 / top)).astype(BF16).reshape(rows, BLK)
        scales[m, 0] = top.reshape(rows // BLK, 1)


def local(tokens, expert_ids, route_weights, placement_of, gate_weight, up_weight, down_weight):
    n_dp, n_z = lax.axis_size("dp"), lax.axis_size("mp")
    nc = n_dp // 2
    n_e, dr, _ = gate_weight.shape
    tg, wide = tokens.shape
    top = expert_ids.shape[1]
    dc, per, lanes = 2 * dr, wide // (2 * dr), NX * tg
    slots = n_e * CAP

    order = jnp.arange(n_e, dtype=jnp.int32)
    inv = jnp.sum(jnp.where(placement_of[:, None] == order[None, :], order[:, None], 0), axis=0)

    vm = pltpu.VMEM
    dma = pltpu.SemaphoreType.DMA
    hbm = pl.BlockSpec(memory_space=pl.ANY)
    vmem = pl.BlockSpec(memory_space=pltpu.VMEM)
    weights = [vm((n_e, dr, BLK), BF16)] * 6
    fresh, mix = pl.pallas_call(
        routed_kernel,
        out_shape=(
            jax.ShapeDtypeStruct((NY, NX, 2, 3, dr, BLK), BF16),
            jax.ShapeDtypeStruct((tg, wide), BF16),
        ),
        in_specs=[pl.BlockSpec(memory_space=pltpu.SMEM), vmem, vmem, vmem, hbm, hbm, hbm],
        out_specs=(hbm, vmem),
        scratch_shapes=weights
        + [
            vm((NY, NX, 2, 3, dr, BLK), BF16),
            vm((NX, NY, 2, 3, dr // 2, BLK), BF16),
            vm((NY, NX, 2, 3, dr // 2, BLK), BF16),
            vm((per, tg, dc), BF16),
            vm((nc, top, lanes), jnp.int32),
            vm((NY, n_e, lanes), F32),
            vm((slots, BLK), F32),
            vm((nc, tg, dc), BF16),
            vm((nc, tg, dc), BF16),
            vm((n_e, NY, NX * CAP, dc), BF16),
            vm((NY, NX, slots, 2 * BLK), BF16),
            vm((NX - 1, NY, slots, BLK), BF16),
            vm((NY - 1, NX, slots, BLK), BF16),
            vm((NY, slots, BLK), BF16),
            vm((NX, slots, BLK), BF16),
            vm((NY - 1, slots, BLK), BF16),
            vm((NX - 1, slots, BLK), BF16),
            vm((NY, NX, slots, BLK), BF16),
            vm((nc, tg, dc), BF16),
            vm((nc, tg, dc), BF16),
            vm((n_z, per, tg, dc), BF16),
            dma((6,)),
            dma((nc,)), dma((nc,)),
            dma((n_z,)), dma((n_z,)),
            dma((nc,)), dma((nc,)),
            dma((3,)), dma((3,)),
            dma((2, NCH, 3)), dma((2, NCH, 3)),
            dma((2, NCH, 3)), dma((2, NCH, 3)),
            dma((NCH, 4)), dma((NCH, 4, 4)), dma((NCH, nc)),
            dma((nc,)), dma((nc,)),
            dma((n_z,)), dma((n_z,)),
            dma((2, 3)), dma((2, 3)),
            dma((2, 4, 2)), dma((2, 4, 2)),
        ],
        compiler_params=pltpu.CompilerParams(collective_id=0, has_side_effects=True, vmem_limit_bytes=62 * 1024 * 1024),
    )(inv, expert_ids.T, route_weights.T, tokens, gate_weight, up_weight, down_weight)
    fresh = fresh.reshape(n_dp, 3, dr, BLK)

    step = max(1, BLK // dr if dr < BLK else 4)
    rows = step * dr
    grid = n_dp // step
    out_w = jax.ShapeDtypeStruct((1, n_dp * dr, BLK), BF16)
    spec_w = pl.BlockSpec((1, rows, BLK), lambda i: (0, i, 0))
    gate_q, up_q, down_q, scales = pl.pallas_call(
        quantize_kernel,
        grid=(grid,),
        out_shape=(out_w, out_w, out_w, jax.ShapeDtypeStruct((3, grid, rows // BLK, 1), F32)),
        in_specs=[pl.BlockSpec((step, 3, dr, BLK), lambda i: (i, 0, 0, 0))],
        out_specs=(spec_w, spec_w, spec_w, pl.BlockSpec((3, 1, rows // BLK, 1), lambda i: (0, i, 0, 0))),
    )(fresh)
    scales = scales.reshape(3, 1, -1, 1)

    return gate_q, up_q, down_q, scales, mix


def solution(mesh):
    placed = (
        P("dp", "mp"),
        P("dp", None),
        P("dp", None),
        P(),
        P(None, "dp", "mp"),
        P(None, "dp", "mp"),
        P(None, "dp", "mp"),
    )
    return jax.shard_map(
        local,
        mesh=mesh,
        in_specs=placed,
        out_specs=(
            P("dp", None, "mp"),
            P("dp", None, "mp"),
            P("dp", None, "mp"),
            P(None, "dp", None, "mp"),
            P("dp", "mp"),
        ),
        check_vma=False,
    )
```

```python
import jax
import jax.numpy as jnp
from jax import lax
from jax.experimental import pallas as pl
from jax.experimental.pallas import tpu as pltpu
from jax.sharding import PartitionSpec as P

BLK = 128
CAP = 24
EPS = 1e-06
NY, NX = 4, 4
NCH = 4
EARLY = 1
MESH = pl.DeviceIdType.MESH
F32, BF16 = jnp.float32, jnp.bfloat16


def routed_kernel(
    inv, ids, rw, tok, wg, wu, wd,
    fresh, mix,
    wog, wou, wod, wsg, wsu, wsd, packed, st_a, st_b, tokp, ids_all, pos_all, slot_w, xs, xg, part,
    hg, hu, rg, ru, qg, qu, r2g, r2u, hid, outp, zb, fin, ob,
    loc, ids_s, ids_r, z_s, z_r, t_s, t_r, w_s, w_r, r0_s, r0_r, r1_s, r1_r, r2_s, r2_r,
    a1_s, a1_r, a2_s, a2_r, a3_s, a3_r, zo_s, zo_r, m_s, m_r, f1_s, f1_r, f2_s, f2_r,
):
    dp, j = lax.axis_index("dp"), lax.axis_index("mp")
    n_dp, n_z = lax.axis_size("dp"), lax.axis_size("mp")
    nc = NX * NY
    c, h = dp // 2, dp % 2
    y, x = c // NX, c % NX
    sib = 2 * c + 1 - h
    n_e, dr, _ = wog.shape
    per = nc // n_z
    home = c // per
    top, tg = ids.shape
    lanes = NX * tg
    eb = n_e // NCH
    rows_ch = eb * CAP
    slots = n_e * CAP
    dc = 2 * dr

    def at(chip):
        return {"dp": 2 * chip + h, "mp": j}

    def remote(src, dst, ss, rs, dev):
        return pltpu.make_async_remote_copy(src_ref=src, dst_ref=dst, send_sem=ss, recv_sem=rs, device_id=dev, device_id_type=MESH)

    own_w = [pltpu.make_async_copy(a, b, loc.at[i]) for i, (a, b) in enumerate(((wg, wog), (wu, wou), (wd, wod)))]
    for cp in own_w:
        cp.start()
    for i in range(per):
        tokp[i] = tok[:, i * dc : (i + 1) * dc]

    lane_g = sum([(lax.broadcasted_iota(jnp.int32, (1, lanes), 1) >= i * tg).astype(jnp.int32) for i in range(1, NX)], jnp.zeros((1, lanes), jnp.int32))
    mine = jnp.where(lane_g == x, jnp.concatenate([ids[...]] * NX, axis=1), -1)
    ids_all[c] = mine

    barrier = pltpu.get_barrier_semaphore()

    def greet(k, _):
        pl.semaphore_signal(barrier, inc=1, device_id={"dp": (dp + k) % n_dp, "mp": j}, device_id_type=MESH)
        return 0

    lax.fori_loop(1, n_dp, greet, 0)

    def greet_z(k, _):
        pl.semaphore_signal(barrier, inc=1, device_id={"dp": dp, "mp": (j + k) % n_z}, device_id_type=MESH)
        return 0

    lax.fori_loop(1, n_z, greet_z, 0)
    for i in range(per):

        @pl.when(per * j + i != c)
        def _():
            pl.semaphore_signal(barrier, inc=1, device_id={"dp": 2 * (per * j + i) + h, "mp": home}, device_id_type=MESH)

    pl.semaphore_wait(barrier, n_dp + n_z - 2 + per - jnp.where(home == j, 1, 0))

    def t_copy(i):
        return remote(tokp.at[i], xs.at[c], t_s.at[i], t_r.at[c % per], {"dp": 2 * (per * j + i) + h, "mp": home})

    def t_from(i):
        return remote(tokp.at[i], xs.at[per * j + i], t_s.at[i], t_r.at[i], {"dp": 2 * (per * j + i) + h, "mp": home})

    for i in range(per):

        @pl.when(per * j + i != c)
        def _():
            t_copy(i).start()

    @pl.when(home == j)
    def _():
        xs[c] = tokp[c % per]

    def ids_copy(k):
        return remote(ids_all.at[c], ids_all.at[c], ids_s.at[k], ids_r.at[k], at((c + k) % nc))

    def ids_start(k, _):
        ids_copy(k).start()
        return 0

    lax.fori_loop(1, nc, ids_start, 0)
    sib_w = [
        remote(a, b, w_s.at[i], w_r.at[i], {"dp": sib, "mp": j})
        for i, (a, b) in enumerate(((wg, wsg), (wu, wsu), (wd, wsd)))
    ]
    for cp in sib_w:
        cp.start()

    for cp in own_w:
        cp.wait()

    def pack(s, _):
        e = inv[s]
        to = (s // (2 * NX), (s // 2) % NX, s % 2)
        packed[to[0], to[1], to[2], 0] = wog[e]
        packed[to[0], to[1], to[2], 1] = wou[e]
        packed[to[0], to[1], to[2], 2] = wod[e]
        return 0

    lax.fori_loop(0, n_e, pack, 0)
    hr = dr // 2
    top_rows, low_rows = pl.ds(0, hr), pl.ds(hr, hr)

    def f1_copy(k, low):
        if low:
            to = (y + k) % NY
            return remote(packed.at[to, :, :, :, low_rows, :], st_b.at[y], f1_s.at[1, k - 1], f1_r.at[1, k - 1], at(to * NX + x))
        to = (x + k) % NX
        return remote(packed.at[:, to, :, :, top_rows, :], st_a.at[x], f1_s.at[0, k - 1], f1_r.at[0, k - 1], at(y * NX + to))

    def f1_from(k, low):
        if low:
            src = (y + NY - k) % NY
            return remote(packed.at[y, :, :, :, low_rows, :], st_b.at[src], f1_s.at[1, k - 1], f1_r.at[1, k - 1], at(src * NX + x))
        src = (x + NX - k) % NX
        return remote(packed.at[:, x, :, :, top_rows, :], st_a.at[src], f1_s.at[0, k - 1], f1_r.at[0, k - 1], at(y * NX + src))

    f1_own = [
        pltpu.make_async_copy(packed.at[:, x, :, :, top_rows, :], st_a.at[x], loc.at[4]),
        pltpu.make_async_copy(packed.at[y, :, :, :, low_rows, :], st_b.at[y], loc.at[5]),
    ]

    def f2_copy(k, d, low):
        core = (h + d) % 2
        if low:
            to = (x + k) % NX
            return remote(st_b.at[:, to, core], fresh.at[:, x, h, :, low_rows, :], f2_s.at[1, k, d], f2_r.at[1, k, d], {"dp": 2 * (y * NX + to) + core, "mp": j})
        to = (y + k) % NY
        return remote(st_a.at[:, to, core], fresh.at[y, :, h, :, top_rows, :], f2_s.at[0, k, d], f2_r.at[0, k, d], {"dp": 2 * (to * NX + x) + core, "mp": j})

    def f2_from(k, d, low):
        core = (h + d) % 2
        if low:
            src = (x + NX - k) % NX
            return remote(st_b.at[:, x, h], fresh.at[:, src, core, :, low_rows, :], f2_s.at[1, k, d], f2_r.at[1, k, d], {"dp": 2 * (y * NX + src) + core, "mp": j})
        src = (y + NY - k) % NY
        return remote(st_a.at[:, y, h], fresh.at[src, :, core, :, top_rows, :], f2_s.at[0, k, d], f2_r.at[0, k, d], {"dp": 2 * (src * NX + x) + core, "mp": j})

    f2_own = [
        pltpu.make_async_copy(st_a.at[:, y, h], fresh.at[y, :, h, :, top_rows, :], loc.at[4]),
        pltpu.make_async_copy(st_b.at[:, x, h], fresh.at[:, x, h, :, low_rows, :], loc.at[5]),
    ]
    steps = [(k, d) for k in range(max(NX, NY)) for d in range(2) if k or d]

    def f2_start(ks):
        for k, d in steps:
            if k in ks:
                if k < NY:
                    f2_copy(k, d, False).start()
                if k < NX:
                    f2_copy(k, d, True).start()

    for cp in f1_own:
        cp.start()
    for k in range(1, NX):
        f1_copy(k, False).start()
    for k in range(1, NY):
        f1_copy(k, True).start()

    lane_i = lax.broadcasted_iota(jnp.int32, (lanes, lanes), 1)
    row_i = lax.broadcasted_iota(jnp.int32, (lanes, lanes), 0)
    lane_of = sum([(lane_i >= i * tg).astype(jnp.int32) for i in range(1, NX)], jnp.zeros((lanes, lanes), jnp.int32))
    row_of = sum([(row_i >= i * tg).astype(jnp.int32) for i in range(1, NX)], jnp.zeros((lanes, lanes), jnp.int32))
    before = jnp.where((row_i < lane_i) & (lane_of == row_of), 1.0, 0.0).astype(BF16)
    e_iota = lax.broadcasted_iota(jnp.int32, (n_e, lanes), 0)
    rw4 = jnp.concatenate([rw[...]] * NX, axis=1)

    def positions(ids):
        named = jnp.zeros((n_e, lanes), F32)
        for i in range(top):
            named = jnp.where(ids[i : i + 1, :] == e_iota, 1.0, named)
        count = jnp.dot(named.astype(BF16), before, preferred_element_type=F32)
        return jnp.where(named > 0.5, count, -1.0)

    my_pos = positions(mine)
    my_w = jnp.zeros((n_e, lanes), F32)
    for i in range(top):
        my_w = jnp.where(mine[i : i + 1, :] == e_iota, rw4[i : i + 1, :], my_w)
    p_iota = lax.broadcasted_iota(jnp.int32, (CAP, lanes), 0).astype(F32)
    for q in range(NCH):
        pe = my_pos[q * eb : (q + 1) * eb, :].reshape(eb, 1, lanes)
        we = my_w[q * eb : (q + 1) * eb, :].reshape(eb, 1, lanes)
        ws = jnp.sum(jnp.where(pe == p_iota[None], we, 0.0), axis=2, keepdims=True)
        slot_w[q * rows_ch : (q + 1) * rows_ch, :] = jnp.broadcast_to(ws.reshape(rows_ch, 1), (rows_ch, BLK))

    def z_copy(k):
        to = (j + k) % n_z
        held = xs.at[pl.ds(per * j, per)]
        return remote(held, held, z_s.at[k], z_r.at[k], {"dp": dp, "mp": to})

    def z_start(k, _):
        z_copy(k).start()
        return 0

    def z_wait(k, _):
        src = (j + n_z - k) % n_z
        held = xs.at[pl.ds(per * src, per)]
        remote(held, held, z_s.at[k], z_r.at[k], {"dp": dp, "mp": src}).wait_recv()
        return 0

    for i in range(per):

        @pl.when(per * j + i != c)
        def _():
            t_from(i).wait_recv()

    lax.fori_loop(1, n_z, z_start, 0)

    def ids_wait(k, _):
        src = (c + nc - k) % nc
        remote(ids_all.at[src], ids_all.at[src], ids_s.at[k], ids_r.at[k], at(src)).wait_recv()
        return 0

    lax.fori_loop(1, nc, ids_wait, 0)

    def place(b, _):
        ids = ids_all[b * NX]
        for i in range(1, NX):
            ids = jnp.maximum(ids, ids_all[b * NX + i])
        pos_all[b] = positions(ids)
        return 0

    lax.fori_loop(0, NY, place, 0)
    lax.fori_loop(1, n_z, z_wait, 0)
    for cp in sib_w:
        cp.wait_recv()

    for cp in f1_own:
        cp.wait()
    for k in range(1, NX):
        f1_from(k, False).wait_recv()
    for k in range(1, NY):
        f1_from(k, True).wait_recv()
    for cp in f2_own:
        cp.start()
    f2_start(range(EARLY))

    r_iota = lax.broadcasted_iota(jnp.int32, (NX * CAP, lanes), 0)
    r_of = sum([(r_iota >= i * CAP).astype(jnp.int32) for i in range(1, NX)], jnp.zeros((NX * CAP, lanes), jnp.int32))
    want = jnp.where(r_of == lane_g, r_iota - CAP * r_of, -9).astype(F32)

    def one_hot(b, q):
        pe = pos_all[b, pl.ds(pl.multiple_of(q * eb, eb), eb), :].reshape(eb, 1, lanes)
        hot = jnp.where(pe == want[None], 1.0, 0.0).astype(BF16)
        return hot.reshape(eb * NX * CAP, lanes)

    def pick(q, b):
        tokens = xs[pl.ds(b * NX, NX)].reshape(lanes, dc)
        got = jnp.dot(one_hot(b, q), tokens, preferred_element_type=F32)
        xg[pl.ds(q * eb, eb), b] = got.astype(BF16).reshape(eb, NX * CAP, dc)

    def by_core(own, other):
        return jnp.concatenate([jnp.where(h == 0, own, other), jnp.where(h == 0, other, own)], axis=0)

    def project(e):
        a = xg[e].reshape(NY * NX * CAP, dc)
        w = jnp.concatenate([by_core(wog[e], wsg[e]), by_core(wou[e], wsu[e])], axis=1)
        return jnp.dot(a, w, preferred_element_type=F32).reshape(nc, CAP, 2 * BLK)

    def rows_of(q):
        return pl.ds(pl.multiple_of(q * rows_ch, rows_ch), rows_ch)

    hy, hx = NY // 2, NX // 2

    def near(way, up):
        if up:
            return (y + 1) % NY if way == 0 else (y + NY - 1) % NY
        return (x + 1) % NX if way == 0 else (x + NX - 1) % NX

    def chip_near(way, up):
        return near(way, up) * NX + x if up else y * NX + near(way, up)

    def r0_copy(q, way, up):
        if up:
            src, dst = part.at[(y + 2) % NY, pl.ds(way * hx, hx), rows_of(q), pl.ds(BLK, BLK)], hu
        else:
            src, dst = part.at[pl.ds(way * hy, hy), (x + 2) % NX, rows_of(q), pl.ds(0, BLK)], hg
        u = int(up)
        return remote(src, dst.at[way, :, rows_of(q), :], r0_s.at[u, q, way], r0_r.at[u, q, way], at(chip_near(way, up)))

    def r1_copy(q, way, up):
        if up:
            src, dst = part.at[near(way, up), :, rows_of(q), pl.ds(BLK, BLK)], ru
        else:
            src, dst = part.at[:, near(way, up), rows_of(q), pl.ds(0, BLK)], rg
        u = int(up)
        return remote(src, dst.at[way, :, rows_of(q), :], r1_s.at[u, q, way], r1_r.at[u, q, way], at(chip_near(way, up)))

    def pass_on(q):
        rows = rows_of(q)
        for way in range(2):
            r0_copy(q, way, False).wait_recv()
            half_y = pl.ds(way * hy, hy)
            got = part[half_y, near(way, False), rows, pl.ds(0, BLK)].astype(F32) + hg[way, :, rows, :].astype(F32)
            part[half_y, near(way, False), rows, pl.ds(0, BLK)] = got.astype(BF16)
            r1_copy(q, way, False).start()
            r0_copy(q, way, True).wait_recv()
            half_x = pl.ds(way * hx, hx)
            got = part[near(way, True), half_x, rows, pl.ds(BLK, BLK)].astype(F32) + hu[way, :, rows, :].astype(F32)
            part[near(way, True), half_x, rows, pl.ds(BLK, BLK)] = got.astype(BF16)
            r1_copy(q, way, True).start()

    def first(q, _):
        for b in range(NY):
            pick(q, b)

        def pair(i, _):
            e = q * eb + 2 * i
            both = jnp.concatenate([project(e), project(e + 1)], axis=1).astype(BF16)
            part[:, :, pl.ds(pl.multiple_of(e * CAP, 2 * CAP), 2 * CAP), :] = both.reshape(NY, NX, 2 * CAP, 2 * BLK)
            return 0

        lax.fori_loop(0, eb // 2, pair, 0)
        for way in range(2):
            r0_copy(q, way, False).start()
            r0_copy(q, way, True).start()

        @pl.when(q > 0)
        def _():
            pass_on(q - 1)

        return 0

    lax.fori_loop(0, NCH, first, 0)
    pass_on(NCH - 1)

    def r2_copy(q, k, up):
        if up:
            to = (x + k) % NX
            return remote(qu.at[to, rows_of(q), :], r2u.at[k - 1, rows_of(q), :], r2_s.at[1, q, k - 1], r2_r.at[1, q, k - 1], at(y * NX + to))
        to = (y + k) % NY
        return remote(qg.at[to, rows_of(q), :], r2g.at[k - 1, rows_of(q), :], r2_s.at[0, q, k - 1], r2_r.at[0, q, k - 1], at(to * NX + x))

    def second(q, _):
        rows = rows_of(q)
        for way in range(2):
            r1_copy(q, way, False).wait_recv()

        def sum_g(i, _):
            t = part[i, x, rows, pl.ds(0, BLK)].astype(F32)
            for way in range(2):
                t = t + rg[way, i, rows, :].astype(F32)
            qg[i, rows, :] = t.astype(BF16)
            return 0

        lax.fori_loop(0, NY, sum_g, 0)
        for k in range(1, NY):
            r2_copy(q, k, False).start()
        for way in range(2):
            r1_copy(q, way, True).wait_recv()

        def sum_u(i, _):
            t = part[y, i, rows, pl.ds(BLK, BLK)].astype(F32)
            for way in range(2):
                t = t + ru[way, i, rows, :].astype(F32)
            qu[i, rows, :] = t.astype(BF16)
            return 0

        lax.fori_loop(0, NX, sum_u, 0)
        for k in range(1, NX):
            r2_copy(q, k, True).start()
        return 0

    lax.fori_loop(0, NCH, second, 0)

    def line(q_along_x, k):
        if q_along_x:
            return y * NX + (x + k) % NX
        return ((y + k) % NY) * NX + x

    def a1_copy(q, k, along_x):
        sl = hid.at[y, x, rows_of(q), :]
        return remote(sl, sl, a1_s.at[q, k], a1_r.at[q, k], at(line(along_x, k)))

    def a1_from(q, k, along_x):
        src = line(along_x, (NX if along_x else NY) - k)
        sl = hid.at[src // NX, src % NX, rows_of(q), :]
        return remote(sl, sl, a1_s.at[q, k], a1_r.at[q, k], at(src))

    def row_block(along_x, place, rows):
        return hid.at[place, :, rows, :] if along_x else hid.at[:, place, rows, :]

    def a2_copy(q, way, along_x):
        sl = row_block(along_x, y if along_x else x, rows_of(q))
        return remote(sl, sl, a2_s.at[q, way], a2_r.at[q, way], at(chip_near(way, along_x)))

    def a2_from(q, way, along_x):
        sl = row_block(along_x, near(1 - way, along_x), rows_of(q))
        return remote(sl, sl, a2_s.at[q, way], a2_r.at[q, way], at(chip_near(1 - way, along_x)))

    def half_rows(q, way):
        return pl.ds(pl.multiple_of(q * rows_ch + way * (rows_ch // 2), rows_ch // 2), rows_ch // 2)

    def a3_copy(q, way, along_x):
        sl = row_block(along_x, near(1 - way, along_x), half_rows(q, way))
        return remote(sl, sl, a3_s.at[q, way], a3_r.at[q, way], at(chip_near(way, along_x)))

    def a3_from(q, way, along_x):
        sl = row_block(along_x, (y + 2) % NY if along_x else (x + 2) % NX, half_rows(q, way))
        return remote(sl, sl, a3_s.at[q, way], a3_r.at[q, way], at(chip_near(1 - way, along_x)))

    def third(along_x):
        n1 = NX if along_x else NY

        def body(q, _):
            rows = rows_of(q)
            for k in range(1, NY):
                r2_copy(q, k, False).wait_recv()
            for k in range(1, NX):
                r2_copy(q, k, True).wait_recv()
            gate = qg[y, rows, :].astype(F32)
            for k in range(NY - 1):
                gate = gate + r2g[k, rows, :].astype(F32)
            up = qu[x, rows, :].astype(F32)
            for k in range(NX - 1):
                up = up + r2u[k, rows, :].astype(F32)
            value = gate / (1.0 + jnp.exp(-gate)) * up * slot_w[rows, :]
            hid[y, x, rows, :] = value.astype(BF16)
            for k in range(1, n1):
                a1_copy(q, k, along_x).start()
            return 0

        return body

    half = NCH // 2
    lax.fori_loop(0, half, third(True), 0)
    lax.fori_loop(half, NCH, third(False), 0)

    def spread(along_x):
        def body(q, _):
            for k in range(1, NX if along_x else NY):
                a1_from(q, k, along_x).wait_recv()
            for way in range(2):
                a2_copy(q, way, along_x).start()
            return 0

        return body

    def forward(along_x):
        def body(q, _):
            for way in range(2):
                a2_from(q, way, along_x).wait_recv()
                a3_copy(q, way, along_x).start()
            return 0

        return body

    lax.fori_loop(0, half, spread(True), 0)
    lax.fori_loop(half, NCH, spread(False), 0)
    lax.fori_loop(0, half, forward(True), 0)
    lax.fori_loop(half, NCH, forward(False), 0)
    f2_start(range(EARLY, max(NX, NY)))

    def down(along_x):
        def body(q, _):
            for way in range(2):
                a3_from(q, way, along_x).wait_recv()

            def pair(i, _):
                e = q * eb + 2 * i
                both = hid[:, :, pl.ds(pl.multiple_of(e * CAP, 2 * CAP), 2 * CAP), :].astype(F32).reshape(nc, 2 * CAP, BLK)
                for o in range(2):
                    a = both[:, o * CAP : (o + 1) * CAP, :].reshape(nc * CAP, BLK).astype(BF16)
                    w = by_core(wod[e + o], wsd[e + o])
                    got = lax.dot_general(a, w, (((1,), (1,)), ((), ())), preferred_element_type=F32)
                    xg[e + o] = got.astype(BF16).reshape(NY, NX * CAP, dc)
                return 0

            lax.fori_loop(0, eb // 2, pair, 0)
            return 0

        return body

    lax.fori_loop(0, half, down(True), 0)
    lax.fori_loop(half, NCH, down(False), 0)

    per_row = NX // per

    def zo_copy(to):
        k = (to + n_z - j) % n_z
        return remote(outp.at[pl.ds(per * to, per)], zb.at[k], zo_s.at[k], zo_r.at[k], {"dp": dp, "mp": to})

    def from_z(k):
        src = (j + n_z - k) % n_z
        return remote(outp.at[pl.ds(per * src, per)], zb.at[k], zo_s.at[k], zo_r.at[k], {"dp": dp, "mp": src})

    def combine(i, _):
        b = (j // per_row + 1 + i) % NY
        total = jnp.zeros((lanes, dc), F32)
        for q in range(NCH):
            d = xg[pl.ds(q * eb, eb), b].reshape(eb * NX * CAP, dc)
            total = total + lax.dot_general(one_hot(b, q), d, (((0,), (0,)), ((), ())), preferred_element_type=F32)
        outp[pl.ds(b * NX, NX)] = total.astype(BF16).reshape(NX, tg, dc)
        for n in range(per_row):
            to = b * per_row + n

            @pl.when(to != j)
            def _():
                zo_copy(to).start()

        return 0

    lax.fori_loop(0, NY, combine, 0)
    total = outp[pl.ds(per * j, per)].astype(F32)
    for k in range(1, n_z):
        from_z(k).wait_recv()
        total = total + zb[k].astype(F32)
    fin[...] = total.astype(BF16)

    def m_copy(i):
        return remote(fin.at[i], ob.at[c % per], m_s.at[i], m_r.at[c % per], {"dp": 2 * (per * j + i) + h, "mp": home})

    def m_from(i):
        return remote(fin.at[i], ob.at[i], m_s.at[i], m_r.at[i], {"dp": 2 * (per * j + i) + h, "mp": home})

    for i in range(per):

        @pl.when(per * j + i != c)
        def _():
            m_copy(i).start()

    @pl.when(home == j)
    def _():
        ob[c % per] = fin[c % per]

    for i in range(per):

        @pl.when(per * j + i != c)
        def _():
            m_from(i).wait_recv()

    mix[...] = jnp.concatenate([ob[i] for i in range(per)], axis=1)

    for cp in f2_own:
        cp.wait()
    for k, d in steps:
        if k < NY:
            f2_from(k, d, False).wait_recv()
            f2_copy(k, d, False).wait_send()
        if k < NX:
            f2_from(k, d, True).wait_recv()
            f2_copy(k, d, True).wait_send()
    for k in range(1, NX):
        f1_copy(k, False).wait_send()
    for k in range(1, NY):
        f1_copy(k, True).wait_send()
    def z_done(k, _):
        z_copy(k).wait_send()
        zo_copy((j + k) % n_z).wait_send()
        return 0

    lax.fori_loop(1, n_z, z_done, 0)
    for i in range(per):

        @pl.when(per * j + i != c)
        def _():
            t_copy(i).wait_send()
            m_copy(i).wait_send()

    def plane_done(k, _):
        ids_copy(k).wait_send()
        return 0

    lax.fori_loop(1, nc, plane_done, 0)
    for cp in sib_w:
        cp.wait_send()

    def sums_done(q, _):
        for way in range(2):
            for up in (False, True):
                r0_copy(q, way, up).wait_send()
                r1_copy(q, way, up).wait_send()
        for k in range(1, NX):
            r2_copy(q, k, True).wait_send()
        for k in range(1, NY):
            r2_copy(q, k, False).wait_send()
        return 0

    lax.fori_loop(0, NCH, sums_done, 0)

    def hid_done(along_x):
        def body(q, _):
            for k in range(1, NX if along_x else NY):
                a1_copy(q, k, along_x).wait_send()
            for way in range(2):
                a2_copy(q, way, along_x).wait_send()
                a3_copy(q, way, along_x).wait_send()
            return 0

        return body

    lax.fori_loop(0, half, hid_done(True), 0)
    lax.fori_loop(half, NCH, hid_done(False), 0)


def quantize_kernel(fresh, gate, up, down, scales):
    rows = gate.shape[1]
    for m, out in enumerate((gate, up, down)):
        w = fresh[:, m].reshape(rows // BLK, BLK, BLK)
        top = jnp.max(jnp.max(jnp.abs(w), axis=1, keepdims=True).astype(F32), axis=2, keepdims=True) + EPS
        out[0] = (w.astype(F32) * (1.0 / top)).astype(BF16).reshape(rows, BLK)
        scales[m, 0] = top.reshape(rows // BLK, 1)


def local(tokens, expert_ids, route_weights, placement_of, gate_weight, up_weight, down_weight):
    n_dp, n_z = lax.axis_size("dp"), lax.axis_size("mp")
    nc = n_dp // 2
    n_e, dr, _ = gate_weight.shape
    tg, wide = tokens.shape
    top = expert_ids.shape[1]
    dc, per, lanes = 2 * dr, wide // (2 * dr), NX * tg
    slots = n_e * CAP

    order = jnp.arange(n_e, dtype=jnp.int32)
    inv = jnp.sum(jnp.where(placement_of[:, None] == order[None, :], order[:, None], 0), axis=0)

    vm = pltpu.VMEM
    dma = pltpu.SemaphoreType.DMA
    hbm = pl.BlockSpec(memory_space=pl.ANY)
    vmem = pl.BlockSpec(memory_space=pltpu.VMEM)
    weights = [vm((n_e, dr, BLK), BF16)] * 6
    fresh, mix = pl.pallas_call(
        routed_kernel,
        out_shape=(
            jax.ShapeDtypeStruct((NY, NX, 2, 3, dr, BLK), BF16),
            jax.ShapeDtypeStruct((tg, wide), BF16),
        ),
        in_specs=[pl.BlockSpec(memory_space=pltpu.SMEM), vmem, vmem, vmem, hbm, hbm, hbm],
        out_specs=(hbm, vmem),
        scratch_shapes=weights
        + [
            vm((NY, NX, 2, 3, dr, BLK), BF16),
            vm((NX, NY, 2, 3, dr // 2, BLK), BF16),
            vm((NY, NX, 2, 3, dr // 2, BLK), BF16),
            vm((per, tg, dc), BF16),
            vm((nc, top, lanes), jnp.int32),
            vm((NY, n_e, lanes), F32),
            vm((slots, BLK), F32),
            vm((nc, tg, dc), BF16),
            vm((n_e, NY, NX * CAP, dc), BF16),
            vm((NY, NX, slots, 2 * BLK), BF16),
            vm((2, NY // 2, slots, BLK), BF16),
            vm((2, NX // 2, slots, BLK), BF16),
            vm((2, NY, slots, BLK), BF16),
            vm((2, NX, slots, BLK), BF16),
            vm((NY, slots, BLK), BF16),
            vm((NX, slots, BLK), BF16),
            vm((NY - 1, slots, BLK), BF16),
            vm((NX - 1, slots, BLK), BF16),
            vm((NY, NX, slots, BLK), BF16),
            vm((nc, tg, dc), BF16),
            vm((n_z, per, tg, dc), BF16),
            vm((per, tg, dc), BF16),
            vm((per, tg, dc), BF16),
            dma((6,)),
            dma((nc,)), dma((nc,)),
            dma((n_z,)), dma((n_z,)),
            dma((per,)), dma((per,)),
            dma((3,)), dma((3,)),
            dma((2, NCH, 2)), dma((2, NCH, 2)),
            dma((2, NCH, 2)), dma((2, NCH, 2)),
            dma((2, NCH, 3)), dma((2, NCH, 3)),
            dma((NCH, 4)), dma((NCH, 4)),
            dma((NCH, 2)), dma((NCH, 2)),
            dma((NCH, 2)), dma((NCH, 2)),
            dma((n_z,)), dma((n_z,)),
            dma((per,)), dma((per,)),
            dma((2, 3)), dma((2, 3)),
            dma((2, 4, 2)), dma((2, 4, 2)),
        ],
        compiler_params=pltpu.CompilerParams(collective_id=0, has_side_effects=True, vmem_limit_bytes=62 * 1024 * 1024),
    )(inv, expert_ids.T, route_weights.T, tokens, gate_weight, up_weight, down_weight)
    fresh = fresh.reshape(n_dp, 3, dr, BLK)

    step = max(1, BLK // dr if dr < BLK else 4)
    rows = step * dr
    grid = n_dp // step
    out_w = jax.ShapeDtypeStruct((1, n_dp * dr, BLK), BF16)
    spec_w = pl.BlockSpec((1, rows, BLK), lambda i: (0, i, 0))
    gate_q, up_q, down_q, scales = pl.pallas_call(
        quantize_kernel,
        grid=(grid,),
        out_shape=(out_w, out_w, out_w, jax.ShapeDtypeStruct((3, grid, rows // BLK, 1), F32)),
        in_specs=[pl.BlockSpec((step, 3, dr, BLK), lambda i: (i, 0, 0, 0))],
        out_specs=(spec_w, spec_w, spec_w, pl.BlockSpec((3, 1, rows // BLK, 1), lambda i: (0, i, 0, 0))),
    )(fresh)
    scales = scales.reshape(3, 1, -1, 1)

    return gate_q, up_q, down_q, scales, mix


def solution(mesh):
    placed = (
        P("dp", "mp"),
        P("dp", None),
        P("dp", None),
        P(),
        P(None, "dp", "mp"),
        P(None, "dp", "mp"),
        P(None, "dp", "mp"),
    )
    return jax.shard_map(
        local,
        mesh=mesh,
        in_specs=placed,
        out_specs=(
            P("dp", None, "mp"),
            P("dp", None, "mp"),
            P("dp", None, "mp"),
            P(None, "dp", None, "mp"),
            P("dp", "mp"),
        ),
        check_vma=False,
    )
```

```python
import jax
import jax.numpy as jnp
from jax import lax
from jax.experimental import pallas as pl
from jax.experimental.pallas import tpu as pltpu
from jax.sharding import PartitionSpec as P

BLK = 128
CAP = 24
EPS = 1e-06
NY, NX = 4, 4
NCH = 4
REST = NCH + 4
MESH = pl.DeviceIdType.MESH
F32, BF16 = jnp.float32, jnp.bfloat16


def routed_kernel(
    inv, ids, rw, tok, wg, wu, wd,
    fresh, mix,
    wog, wou, wod, wsg, wsu, wsd, packed, st_a, st_b, tokp, ids_all, pos_all, hots, slot_w, xs, xg, part,
    hg, hu, rg, ru, qg, qu, r2g, r2u, hid, outp, zb, fin, ob,
    loc, ids_s, ids_r, z_s, z_r, t_s, t_r, w_s, w_r, r0_s, r0_r, r1_s, r1_r, r2_s, r2_r,
    a1_s, a1_r, a2_s, a2_r, a3_s, a3_r, zo_s, zo_r, m_s, m_r, f1_s, f1_r, f2_s, f2_r,
):
    dp, j = lax.axis_index("dp"), lax.axis_index("mp")
    n_dp, n_z = lax.axis_size("dp"), lax.axis_size("mp")
    nc = NX * NY
    c, h = dp // 2, dp % 2
    y, x = c // NX, c % NX
    sib = 2 * c + 1 - h
    n_e, dr, _ = wog.shape
    per = nc // n_z
    home = c // per
    top, tg = ids.shape
    lanes = NX * tg
    eb = n_e // NCH
    rows_ch = eb * CAP
    slots = n_e * CAP
    dc = 2 * dr

    def at(chip):
        return {"dp": 2 * chip + h, "mp": j}

    def remote(src, dst, ss, rs, dev):
        return pltpu.make_async_remote_copy(src_ref=src, dst_ref=dst, send_sem=ss, recv_sem=rs, device_id=dev, device_id_type=MESH)

    own_w = [pltpu.make_async_copy(a, b, loc.at[i]) for i, (a, b) in enumerate(((wg, wog), (wu, wou), (wd, wod)))]
    for cp in own_w:
        cp.start()
    for i in range(per):
        tokp[i] = tok[:, i * dc : (i + 1) * dc]

    lane_g = sum([(lax.broadcasted_iota(jnp.int32, (1, lanes), 1) >= i * tg).astype(jnp.int32) for i in range(1, NX)], jnp.zeros((1, lanes), jnp.int32))
    mine = jnp.where(lane_g == x, jnp.concatenate([ids[...]] * NX, axis=1), -1)
    ids_all[c] = mine

    barrier = pltpu.get_barrier_semaphore()

    def greet(k, _):
        pl.semaphore_signal(barrier, inc=1, device_id={"dp": (dp + k) % n_dp, "mp": j}, device_id_type=MESH)
        return 0

    lax.fori_loop(1, n_dp, greet, 0)

    def greet_z(k, _):
        pl.semaphore_signal(barrier, inc=1, device_id={"dp": dp, "mp": (j + k) % n_z}, device_id_type=MESH)
        return 0

    lax.fori_loop(1, n_z, greet_z, 0)
    for i in range(per):

        @pl.when(per * j + i != c)
        def _():
            pl.semaphore_signal(barrier, inc=1, device_id={"dp": 2 * (per * j + i) + h, "mp": home}, device_id_type=MESH)

    for cp in own_w:
        cp.wait()

    def pack(s, _):
        e = inv[s]
        to = (s // (2 * NX), (s // 2) % NX, s % 2)
        packed[to[0], to[1], to[2], 0] = wog[e]
        packed[to[0], to[1], to[2], 1] = wou[e]
        packed[to[0], to[1], to[2], 2] = wod[e]
        return 0

    lax.fori_loop(0, n_e, pack, 0)
    pl.semaphore_wait(barrier, n_dp + n_z - 2 + per - jnp.where(home == j, 1, 0))

    def t_copy(i):
        return remote(tokp.at[i], xs.at[c], t_s.at[i], t_r.at[c % per], {"dp": 2 * (per * j + i) + h, "mp": home})

    def t_from(i):
        return remote(tokp.at[i], xs.at[per * j + i], t_s.at[i], t_r.at[i], {"dp": 2 * (per * j + i) + h, "mp": home})

    for i in range(per):

        @pl.when(per * j + i != c)
        def _():
            t_copy(i).start()

    @pl.when(home == j)
    def _():
        xs[c] = tokp[c % per]

    def ids_copy(k):
        return remote(ids_all.at[c], ids_all.at[c], ids_s.at[k], ids_r.at[k], at((c + k) % nc))

    def ids_start(k, _):
        ids_copy(k).start()
        return 0

    lax.fori_loop(1, nc, ids_start, 0)
    sib_w = [
        remote(a, b, w_s.at[i], w_r.at[i], {"dp": sib, "mp": j})
        for i, (a, b) in enumerate(((wg, wsg), (wu, wsu), (wd, wsd)))
    ]
    for cp in sib_w:
        cp.start()

    hr = dr // 2
    top_rows, low_rows = pl.ds(0, hr), pl.ds(hr, hr)

    def f1_copy(k, low):
        if low:
            to = (y + k) % NY
            return remote(packed.at[to, :, :, :, low_rows, :], st_b.at[y], f1_s.at[1, k - 1], f1_r.at[1, k - 1], at(to * NX + x))
        to = (x + k) % NX
        return remote(packed.at[:, to, :, :, top_rows, :], st_a.at[x], f1_s.at[0, k - 1], f1_r.at[0, k - 1], at(y * NX + to))

    def f1_from(k, low):
        if low:
            src = (y + NY - k) % NY
            return remote(packed.at[y, :, :, :, low_rows, :], st_b.at[src], f1_s.at[1, k - 1], f1_r.at[1, k - 1], at(src * NX + x))
        src = (x + NX - k) % NX
        return remote(packed.at[:, x, :, :, top_rows, :], st_a.at[src], f1_s.at[0, k - 1], f1_r.at[0, k - 1], at(y * NX + src))

    f1_own = [
        pltpu.make_async_copy(packed.at[:, x, :, :, top_rows, :], st_a.at[x], loc.at[4]),
        pltpu.make_async_copy(packed.at[y, :, :, :, low_rows, :], st_b.at[y], loc.at[5]),
    ]

    def f2_copy(k, d, low):
        core = (h + d) % 2
        if low:
            to = (x + k) % NX
            return remote(st_b.at[:, to, core], fresh.at[:, x, h, :, low_rows, :], f2_s.at[1, k, d], f2_r.at[1, k, d], {"dp": 2 * (y * NX + to) + core, "mp": j})
        to = (y + k) % NY
        return remote(st_a.at[:, to, core], fresh.at[y, :, h, :, top_rows, :], f2_s.at[0, k, d], f2_r.at[0, k, d], {"dp": 2 * (to * NX + x) + core, "mp": j})

    def f2_from(k, d, low):
        core = (h + d) % 2
        if low:
            src = (x + NX - k) % NX
            return remote(st_b.at[:, x, h], fresh.at[:, src, core, :, low_rows, :], f2_s.at[1, k, d], f2_r.at[1, k, d], {"dp": 2 * (y * NX + src) + core, "mp": j})
        src = (y + NY - k) % NY
        return remote(st_a.at[:, y, h], fresh.at[src, :, core, :, top_rows, :], f2_s.at[0, k, d], f2_r.at[0, k, d], {"dp": 2 * (src * NX + x) + core, "mp": j})

    f2_own = [
        pltpu.make_async_copy(st_a.at[:, y, h], fresh.at[y, :, h, :, top_rows, :], loc.at[4]),
        pltpu.make_async_copy(st_b.at[:, x, h], fresh.at[:, x, h, :, low_rows, :], loc.at[5]),
    ]
    steps = [(k, d) for k in range(max(NX, NY)) for d in range(2) if k or d]

    def f2_start(ks):
        for k, d in steps:
            if k in ks:
                if k < NY:
                    f2_copy(k, d, False).start()
                if k < NX:
                    f2_copy(k, d, True).start()

    for cp in f1_own:
        cp.start()
    for k in range(1, NX):
        f1_copy(k, False).start()
    for k in range(1, NY):
        f1_copy(k, True).start()

    lane_i = lax.broadcasted_iota(jnp.int32, (lanes, lanes), 1)
    row_i = lax.broadcasted_iota(jnp.int32, (lanes, lanes), 0)
    lane_of = sum([(lane_i >= i * tg).astype(jnp.int32) for i in range(1, NX)], jnp.zeros((lanes, lanes), jnp.int32))
    row_of = sum([(row_i >= i * tg).astype(jnp.int32) for i in range(1, NX)], jnp.zeros((lanes, lanes), jnp.int32))
    before = jnp.where((row_i < lane_i) & (lane_of == row_of), 1.0, 0.0).astype(BF16)
    e_iota = lax.broadcasted_iota(jnp.int32, (n_e, lanes), 0)
    rw4 = jnp.concatenate([rw[...]] * NX, axis=1)

    def positions(ids):
        named = jnp.zeros((n_e, lanes), F32)
        for i in range(top):
            named = jnp.where(ids[i : i + 1, :] == e_iota, 1.0, named)
        count = jnp.dot(named.astype(BF16), before, preferred_element_type=F32)
        return jnp.where(named > 0.5, count, -1.0)

    my_pos = positions(mine)
    my_w = jnp.zeros((n_e, lanes), F32)
    for i in range(top):
        my_w = jnp.where(mine[i : i + 1, :] == e_iota, rw4[i : i + 1, :], my_w)
    p_iota = lax.broadcasted_iota(jnp.int32, (CAP, lanes), 0).astype(F32)
    for q in range(NCH):
        pe = my_pos[q * eb : (q + 1) * eb, :].reshape(eb, 1, lanes)
        we = my_w[q * eb : (q + 1) * eb, :].reshape(eb, 1, lanes)
        ws = jnp.sum(jnp.where(pe == p_iota[None], we, 0.0), axis=2, keepdims=True)
        slot_w[q * rows_ch : (q + 1) * rows_ch, :] = jnp.broadcast_to(ws.reshape(rows_ch, 1), (rows_ch, BLK))

    far = n_z // 2
    hp = per // 2

    def z_copy(s, way):
        src = (j + n_z - s) % n_z if way == 0 else (j + s) % n_z
        to = (j + 1) % n_z if way == 0 else (j + n_z - 1) % n_z
        held = xs.at[pl.ds(per * src + way * hp, hp)] if s == far - 1 else xs.at[pl.ds(per * src, per)]
        return remote(held, held, z_s.at[way, s], z_r.at[way, s], {"dp": dp, "mp": to})

    def z_from(s, way):
        src = (j + n_z - s - 1) % n_z if way == 0 else (j + s + 1) % n_z
        to = (j + n_z - 1) % n_z if way == 0 else (j + 1) % n_z
        held = xs.at[pl.ds(per * src + way * hp, hp)] if s == far - 1 else xs.at[pl.ds(per * src, per)]
        return remote(held, held, z_s.at[way, s], z_r.at[way, s], {"dp": dp, "mp": to})

    for i in range(per):

        @pl.when(per * j + i != c)
        def _():
            t_from(i).wait_recv()

    for way in range(2):
        z_copy(0, way).start()

    def ids_wait(k, _):
        src = (c + nc - k) % nc
        remote(ids_all.at[src], ids_all.at[src], ids_s.at[k], ids_r.at[k], at(src)).wait_recv()
        return 0

    lax.fori_loop(1, nc, ids_wait, 0)

    r_iota = lax.broadcasted_iota(jnp.int32, (NX * CAP, lanes), 0)
    r_of = sum([(r_iota >= i * CAP).astype(jnp.int32) for i in range(1, NX)], jnp.zeros((NX * CAP, lanes), jnp.int32))
    want = jnp.where(r_of == lane_g, r_iota - CAP * r_of, -9).astype(F32)

    def place(b, _):
        ids = ids_all[b * NX]
        for i in range(1, NX):
            ids = jnp.maximum(ids, ids_all[b * NX + i])
        pos_all[b] = positions(ids)

        def hot(q, _):
            pe = pos_all[b, pl.ds(pl.multiple_of(q * eb, eb), eb), :].reshape(eb, 1, lanes)
            hots[b, q] = jnp.where(pe == want[None], 1.0, 0.0).astype(BF16).reshape(eb * NX * CAP, lanes)
            return 0

        return lax.fori_loop(0, NCH, hot, 0)

    for s in range(1, far):
        lax.fori_loop(NY * (s - 1) // (far - 1), NY * s // (far - 1), place, 0)
        for way in range(2):
            z_from(s - 1, way).wait_recv()
            z_copy(s, way).start()
    for way in range(2):
        z_from(far - 1, way).wait_recv()
    for cp in sib_w:
        cp.wait_recv()


    def pick(q, b):
        tokens = xs[pl.ds(b * NX, NX)].reshape(lanes, dc)
        got = jnp.dot(hots[b, q], tokens, preferred_element_type=F32)
        xg[pl.ds(q * eb, eb), b] = got.astype(BF16).reshape(eb, NX * CAP, dc)

    def by_core(own, other):
        return jnp.concatenate([jnp.where(h == 0, own, other), jnp.where(h == 0, other, own)], axis=0)

    def project(e):
        a = xg[e].reshape(NY * NX * CAP, dc)
        w = jnp.concatenate([by_core(wog[e], wsg[e]), by_core(wou[e], wsu[e])], axis=1)
        return jnp.dot(a, w, preferred_element_type=F32).reshape(nc, CAP, 2 * BLK)

    def rows_of(q):
        return pl.ds(pl.multiple_of(q * rows_ch, rows_ch), rows_ch)

    hy, hx = NY // 2, NX // 2

    def near(way, up):
        if up:
            return (y + 1) % NY if way == 0 else (y + NY - 1) % NY
        return (x + 1) % NX if way == 0 else (x + NX - 1) % NX

    def chip_near(way, up):
        return near(way, up) * NX + x if up else y * NX + near(way, up)

    def r0_copy(q, way, up):
        if up:
            src, dst = part.at[(y + 2) % NY, pl.ds(way * hx, hx), rows_of(q), pl.ds(BLK, BLK)], hu
        else:
            src, dst = part.at[pl.ds(way * hy, hy), (x + 2) % NX, rows_of(q), pl.ds(0, BLK)], hg
        u = int(up)
        return remote(src, dst.at[way, :, rows_of(q), :], r0_s.at[u, q, way], r0_r.at[u, q, way], at(chip_near(way, up)))

    def r1_copy(q, way, up):
        if up:
            src, dst = part.at[near(way, up), :, rows_of(q), pl.ds(BLK, BLK)], ru
        else:
            src, dst = part.at[:, near(way, up), rows_of(q), pl.ds(0, BLK)], rg
        u = int(up)
        return remote(src, dst.at[way, :, rows_of(q), :], r1_s.at[u, q, way], r1_r.at[u, q, way], at(chip_near(way, up)))

    def pass_on(q):
        rows = rows_of(q)
        for way in range(2):
            r0_copy(q, way, False).wait_recv()
            half_y = pl.ds(way * hy, hy)
            got = part[half_y, near(way, False), rows, pl.ds(0, BLK)].astype(F32) + hg[way, :, rows, :].astype(F32)
            part[half_y, near(way, False), rows, pl.ds(0, BLK)] = got.astype(BF16)
            r1_copy(q, way, False).start()
            r0_copy(q, way, True).wait_recv()
            half_x = pl.ds(way * hx, hx)
            got = part[near(way, True), half_x, rows, pl.ds(BLK, BLK)].astype(F32) + hu[way, :, rows, :].astype(F32)
            part[near(way, True), half_x, rows, pl.ds(BLK, BLK)] = got.astype(BF16)
            r1_copy(q, way, True).start()

    def first(q):
        for b in range(NY):
            pick(q, b)

        def pair(i, _):
            e = q * eb + 2 * i
            both = jnp.concatenate([project(e), project(e + 1)], axis=1).astype(BF16)
            part[:, :, pl.ds(pl.multiple_of(e * CAP, 2 * CAP), 2 * CAP), :] = both.reshape(NY, NX, 2 * CAP, 2 * BLK)
            return 0

        lax.fori_loop(0, eb // 2, pair, 0)
        for way in range(2):
            r0_copy(q, way, False).start()
            r0_copy(q, way, True).start()

        return 0

    def r2_copy(q, k, up):
        if up:
            to = (x + k) % NX
            return remote(qu.at[to, rows_of(q), :], r2u.at[k - 1, rows_of(q), :], r2_s.at[1, q, k - 1], r2_r.at[1, q, k - 1], at(y * NX + to))
        to = (y + k) % NY
        return remote(qg.at[to, rows_of(q), :], r2g.at[k - 1, rows_of(q), :], r2_s.at[0, q, k - 1], r2_r.at[0, q, k - 1], at(to * NX + x))

    def second(q):
        rows = rows_of(q)
        for way in range(2):
            r1_copy(q, way, False).wait_recv()

        def sum_g(i, _):
            t = part[i, x, rows, pl.ds(0, BLK)].astype(F32)
            for way in range(2):
                t = t + rg[way, i, rows, :].astype(F32)
            qg[i, rows, :] = t.astype(BF16)
            return 0

        lax.fori_loop(0, NY, sum_g, 0)
        for k in range(1, NY):
            r2_copy(q, k, False).start()
        for way in range(2):
            r1_copy(q, way, True).wait_recv()

        def sum_u(i, _):
            t = part[y, i, rows, pl.ds(BLK, BLK)].astype(F32)
            for way in range(2):
                t = t + ru[way, i, rows, :].astype(F32)
            qu[i, rows, :] = t.astype(BF16)
            return 0

        lax.fori_loop(0, NX, sum_u, 0)
        for k in range(1, NX):
            r2_copy(q, k, True).start()
        return 0


    def line(q_along_x, k):
        if q_along_x:
            return y * NX + (x + k) % NX
        return ((y + k) % NY) * NX + x

    hr_ch = rows_ch // 2

    def half_of(q, along_x, part_of=None):
        start, size = q * rows_ch + (0 if along_x else hr_ch), hr_ch
        if part_of is not None:
            start, size = start + part_of * (hr_ch // 2), hr_ch // 2
        return pl.ds(pl.multiple_of(start, hr_ch // 2), size)

    def a1_copy(q, k, along_x):
        sl = hid.at[y, x, half_of(q, along_x), :]
        u = int(along_x)
        return remote(sl, sl, a1_s.at[u, q, k], a1_r.at[u, q, k], at(line(along_x, k)))

    def a1_from(q, k, along_x):
        src = line(along_x, (NX if along_x else NY) - k)
        sl = hid.at[src // NX, src % NX, half_of(q, along_x), :]
        u = int(along_x)
        return remote(sl, sl, a1_s.at[u, q, k], a1_r.at[u, q, k], at(src))

    def row_block(along_x, place, rows):
        return hid.at[place, :, rows, :] if along_x else hid.at[:, place, rows, :]

    def a2_copy(q, way, along_x):
        sl = row_block(along_x, y if along_x else x, half_of(q, along_x))
        u = int(along_x)
        return remote(sl, sl, a2_s.at[u, q, way], a2_r.at[u, q, way], at(chip_near(way, along_x)))

    def a2_from(q, way, along_x):
        sl = row_block(along_x, near(1 - way, along_x), half_of(q, along_x))
        u = int(along_x)
        return remote(sl, sl, a2_s.at[u, q, way], a2_r.at[u, q, way], at(chip_near(1 - way, along_x)))

    def a3_copy(q, way, along_x):
        sl = row_block(along_x, near(1 - way, along_x), half_of(q, along_x, way))
        u = int(along_x)
        return remote(sl, sl, a3_s.at[u, q, way], a3_r.at[u, q, way], at(chip_near(way, along_x)))

    def a3_from(q, way, along_x):
        sl = row_block(along_x, (y + 2) % NY if along_x else (x + 2) % NX, half_of(q, along_x, way))
        u = int(along_x)
        return remote(sl, sl, a3_s.at[u, q, way], a3_r.at[u, q, way], at(chip_near(1 - way, along_x)))

    def third(q):
        rows = rows_of(q)
        for k in range(1, NY):
            r2_copy(q, k, False).wait_recv()
        for k in range(1, NX):
            r2_copy(q, k, True).wait_recv()
        gate = qg[y, rows, :].astype(F32)
        for k in range(NY - 1):
            gate = gate + r2g[k, rows, :].astype(F32)
        up = qu[x, rows, :].astype(F32)
        for k in range(NX - 1):
            up = up + r2u[k, rows, :].astype(F32)
        value = gate / (1.0 + jnp.exp(-gate)) * up * slot_w[rows, :]
        hid[y, x, rows, :] = value.astype(BF16)
        for k in range(1, NX):
            a1_copy(q, k, True).start()
        for k in range(1, NY):
            a1_copy(q, k, False).start()

    def spread(q):
        for along_x in (True, False):
            for k in range(1, NX if along_x else NY):
                a1_from(q, k, along_x).wait_recv()
            for way in range(2):
                a2_copy(q, way, along_x).start()

    def forward(q):
        for along_x in (True, False):
            for way in range(2):
                a2_from(q, way, along_x).wait_recv()
                a3_copy(q, way, along_x).start()

    def down(q):
        for along_x in (True, False):
            for way in range(2):
                a3_from(q, way, along_x).wait_recv()

        def pair(i, _):
            e = q * eb + 2 * i
            both = hid[:, :, pl.ds(pl.multiple_of(e * CAP, 2 * CAP), 2 * CAP), :].astype(F32).reshape(nc, 2 * CAP, BLK)
            for o in range(2):
                a = both[:, o * CAP : (o + 1) * CAP, :].reshape(nc * CAP, BLK).astype(BF16)
                w = by_core(wod[e + o], wsd[e + o])
                got = lax.dot_general(a, w, (((1,), (1,)), ((), ())), preferred_element_type=F32)
                xg[e + o] = got.astype(BF16).reshape(NY, NX * CAP, dc)
            return 0

        lax.fori_loop(0, eb // 2, pair, 0)

    stages = [first]
    stages += [pass_on, second]
    stages += [third]
    stages += [spread, forward, down]

    def beat(t, _):
        for n, stage in enumerate(stages):

            @pl.when((t >= n) & (t < n + NCH))
            def _():
                stage(t - n)

        @pl.when(t == REST)
        def _():
            for cp in f1_own:
                cp.wait()
            for k in range(1, NX):
                f1_from(k, False).wait_recv()
            for k in range(1, NY):
                f1_from(k, True).wait_recv()
            for cp in f2_own:
                cp.start()
            f2_start(range(max(NX, NY)))

        return 0

    lax.fori_loop(0, NCH + len(stages) - 1, beat, 0)
    per_row = NX // per

    def zo_copy(to, n):
        k = (to + n_z - j) % n_z
        return remote(outp.at[per * to + n], zb.at[n, k], zo_s.at[n, k], zo_r.at[n, k], {"dp": dp, "mp": to})

    def from_z(k, n):
        src = (j + n_z - k) % n_z
        return remote(outp.at[per * src + n], zb.at[n, k], zo_s.at[n, k], zo_r.at[n, k], {"dp": dp, "mp": src})

    def combine(i, _):
        b = (j // per_row + 1 + i) % NY
        total = jnp.zeros((lanes, dc), F32)
        for q in range(NCH):
            d = xg[pl.ds(q * eb, eb), b].reshape(eb * NX * CAP, dc)
            total = total + lax.dot_general(hots[b, q], d, (((0,), (0,)), ((), ())), preferred_element_type=F32)
        outp[pl.ds(b * NX, NX)] = total.astype(BF16).reshape(NX, tg, dc)
        for n in range(per_row):
            to = b * per_row + n

            @pl.when(to != j)
            def _():
                zo_copy(to, 0).start()

        return 0

    lax.fori_loop(0, NY, combine, 0)
    def zo_start(k, _):
        for n in range(1, per):
            zo_copy((j + k) % n_z, n).start()
        return 0

    lax.fori_loop(1, n_z, zo_start, 0)

    def m_copy(i):
        return remote(fin.at[i], ob.at[c % per], m_s.at[i], m_r.at[c % per], {"dp": 2 * (per * j + i) + h, "mp": home})

    def m_from(i):
        return remote(fin.at[i], ob.at[i], m_s.at[i], m_r.at[i], {"dp": 2 * (per * j + i) + h, "mp": home})

    for i in range(per):
        total = outp[per * j + i].astype(F32)
        for k in range(1, n_z):
            from_z(k, i).wait_recv()
            total = total + zb[i, k].astype(F32)
        fin[i] = total.astype(BF16)

        @pl.when(per * j + i != c)
        def _():
            m_copy(i).start()

    @pl.when(home == j)
    def _():
        ob[c % per] = fin[c % per]

    for i in range(per):

        @pl.when(per * j + i != c)
        def _():
            m_from(i).wait_recv()

    mix[...] = jnp.concatenate([ob[i] for i in range(per)], axis=1)

    for cp in f2_own:
        cp.wait()
    for k, d in steps:
        if k < NY:
            f2_from(k, d, False).wait_recv()
            f2_copy(k, d, False).wait_send()
        if k < NX:
            f2_from(k, d, True).wait_recv()
            f2_copy(k, d, True).wait_send()
    for k in range(1, NX):
        f1_copy(k, False).wait_send()
    for k in range(1, NY):
        f1_copy(k, True).wait_send()
    def z_done(k, _):
        for n in range(per):
            zo_copy((j + k) % n_z, n).wait_send()
        return 0

    lax.fori_loop(1, n_z, z_done, 0)
    for s in range(far):
        for way in range(2):
            z_copy(s, way).wait_send()
    for i in range(per):

        @pl.when(per * j + i != c)
        def _():
            t_copy(i).wait_send()
            m_copy(i).wait_send()

    def plane_done(k, _):
        ids_copy(k).wait_send()
        return 0

    lax.fori_loop(1, nc, plane_done, 0)
    for cp in sib_w:
        cp.wait_send()

    def sums_done(q, _):
        for way in range(2):
            for up in (False, True):
                r0_copy(q, way, up).wait_send()
                r1_copy(q, way, up).wait_send()
        for k in range(1, NX):
            r2_copy(q, k, True).wait_send()
        for k in range(1, NY):
            r2_copy(q, k, False).wait_send()
        return 0

    lax.fori_loop(0, NCH, sums_done, 0)

    def hid_done(q, _):
        for along_x in (True, False):
            for k in range(1, NX if along_x else NY):
                a1_copy(q, k, along_x).wait_send()
            for way in range(2):
                a2_copy(q, way, along_x).wait_send()
                a3_copy(q, way, along_x).wait_send()
        return 0

    lax.fori_loop(0, NCH, hid_done, 0)


def quantize_kernel(fresh, gate, up, down, scales):
    rows = gate.shape[1]
    for m, out in enumerate((gate, up, down)):
        w = fresh[:, m].reshape(rows // BLK, BLK, BLK).astype(F32)
        top = jnp.max(jnp.max(jnp.abs(w), axis=1, keepdims=True), axis=2, keepdims=True) + EPS
        out[0] = (w * (1.0 / top)).astype(BF16).reshape(rows, BLK)
        scales[m, 0] = top.reshape(rows // BLK, 1)


def local(tokens, expert_ids, route_weights, placement_of, gate_weight, up_weight, down_weight):
    n_dp, n_z = lax.axis_size("dp"), lax.axis_size("mp")
    nc = n_dp // 2
    n_e, dr, _ = gate_weight.shape
    tg, wide = tokens.shape
    top = expert_ids.shape[1]
    dc, per, lanes = 2 * dr, wide // (2 * dr), NX * tg
    slots = n_e * CAP

    order = jnp.arange(n_e, dtype=jnp.int32)
    inv = jnp.sum(jnp.where(placement_of[:, None] == order[None, :], order[:, None], 0), axis=0)

    vm = pltpu.VMEM
    dma = pltpu.SemaphoreType.DMA
    hbm = pl.BlockSpec(memory_space=pl.ANY)
    vmem = pl.BlockSpec(memory_space=pltpu.VMEM)
    weights = [vm((n_e, dr, BLK), BF16)] * 6
    fresh, mix = pl.pallas_call(
        routed_kernel,
        out_shape=(
            jax.ShapeDtypeStruct((NY, NX, 2, 3, dr, BLK), BF16),
            jax.ShapeDtypeStruct((tg, wide), BF16),
        ),
        in_specs=[pl.BlockSpec(memory_space=pltpu.SMEM), vmem, vmem, vmem, hbm, hbm, hbm],
        out_specs=(hbm, vmem),
        scratch_shapes=weights
        + [
            vm((NY, NX, 2, 3, dr, BLK), BF16),
            vm((NX, NY, 2, 3, dr // 2, BLK), BF16),
            vm((NY, NX, 2, 3, dr // 2, BLK), BF16),
            vm((per, tg, dc), BF16),
            vm((nc, top, lanes), jnp.int32),
            vm((NY, n_e, lanes), F32),
            vm((NY, NCH, slots // NCH * NX, lanes), BF16),
            vm((slots, BLK), F32),
            vm((nc, tg, dc), BF16),
            vm((n_e, NY, NX * CAP, dc), BF16),
            vm((NY, NX, slots, 2 * BLK), BF16),
            vm((2, NY // 2, slots, BLK), BF16),
            vm((2, NX // 2, slots, BLK), BF16),
            vm((2, NY, slots, BLK), BF16),
            vm((2, NX, slots, BLK), BF16),
            vm((NY, slots, BLK), BF16),
            vm((NX, slots, BLK), BF16),
            vm((NY - 1, slots, BLK), BF16),
            vm((NX - 1, slots, BLK), BF16),
            vm((NY, NX, slots, BLK), BF16),
            vm((nc, tg, dc), BF16),
            vm((per, n_z, tg, dc), BF16),
            vm((per, tg, dc), BF16),
            vm((per, tg, dc), BF16),
            dma((6,)),
            dma((nc,)), dma((nc,)),
            dma((2, n_z // 2)), dma((2, n_z // 2)),
            dma((per,)), dma((per,)),
            dma((3,)), dma((3,)),
            dma((2, NCH, 2)), dma((2, NCH, 2)),
            dma((2, NCH, 2)), dma((2, NCH, 2)),
            dma((2, NCH, 3)), dma((2, NCH, 3)),
            dma((2, NCH, 4)), dma((2, NCH, 4)),
            dma((2, NCH, 2)), dma((2, NCH, 2)),
            dma((2, NCH, 2)), dma((2, NCH, 2)),
            dma((per, n_z)), dma((per, n_z)),
            dma((per,)), dma((per,)),
            dma((2, 3)), dma((2, 3)),
            dma((2, 4, 2)), dma((2, 4, 2)),
        ],
        compiler_params=pltpu.CompilerParams(collective_id=0, has_side_effects=True, vmem_limit_bytes=62 * 1024 * 1024),
    )(inv, expert_ids.T, route_weights.T, tokens, gate_weight, up_weight, down_weight)
    fresh = fresh.reshape(n_dp, 3, dr, BLK)

    step = n_dp // 2
    rows = step * dr
    grid = n_dp // step
    out_w = jax.ShapeDtypeStruct((1, n_dp * dr, BLK), BF16)
    spec_w = pl.BlockSpec((1, rows, BLK), lambda i: (0, i, 0))
    gate_q, up_q, down_q, scales = pl.pallas_call(
        quantize_kernel,
        grid=(grid,),
        out_shape=(out_w, out_w, out_w, jax.ShapeDtypeStruct((3, grid, rows // BLK, 1), F32)),
        in_specs=[pl.BlockSpec((step, 3, dr, BLK), lambda i: (i, 0, 0, 0))],
        out_specs=(spec_w, spec_w, spec_w, pl.BlockSpec((3, 1, rows // BLK, 1), lambda i: (0, i, 0, 0))),
        compiler_params=pltpu.CompilerParams(vmem_limit_bytes=48 * 1024 * 1024),
    )(fresh)
    scales = scales.reshape(3, 1, -1, 1)

    return gate_q, up_q, down_q, scales, mix


def solution(mesh):
    placed = (
        P("dp", "mp"),
        P("dp", None),
        P("dp", None),
        P(),
        P(None, "dp", "mp"),
        P(None, "dp", "mp"),
        P(None, "dp", "mp"),
    )
    return jax.shard_map(
        local,
        mesh=mesh,
        in_specs=placed,
        out_specs=(
            P("dp", None, "mp"),
            P("dp", None, "mp"),
            P("dp", None, "mp"),
            P(None, "dp", None, "mp"),
            P("dp", "mp"),
        ),
        check_vma=False,
    )
```

```python
import jax
import jax.numpy as jnp
from jax import lax
from jax.experimental import pallas as pl
from jax.experimental.pallas import tpu as pltpu
from jax.sharding import PartitionSpec as P

BLK = 128
CAP = 24
EPS = 1e-06
NY, NX = 4, 4
NCH = 4
REST = NCH + 6
MESH = pl.DeviceIdType.MESH
F32, BF16 = jnp.float32, jnp.bfloat16


def routed_kernel(
    inv, ids, rw, tok, wg, wu, wd,
    fresh, mix,
    wog, wou, wod, wsg, wsu, wsd, packed, st_a, st_b, tokp, ids_all, hots, places, row_w, xs, xg, part, dens,
    hg, hu, rg, ru, r2g, r2u, hid, zb, fin, ob,
    loc, ids_s, ids_r, z_s, z_r, t_s, t_r, w_s, w_r, r0_s, r0_r, r1_s, r1_r, r2_s, r2_r,
    a1_s, a1_r, a2_s, a2_r, a3_s, a3_r, zo_s, zo_r, m_s, m_r, f1_s, f1_r, f2_s, f2_r,
):
    dp, j = lax.axis_index("dp"), lax.axis_index("mp")
    n_dp, n_z = lax.axis_size("dp"), lax.axis_size("mp")
    nc = NX * NY
    c, h = dp // 2, dp % 2
    y, x = c // NX, c % NX
    sib = 2 * c + 1 - h
    n_e, dr, _ = wog.shape
    per = nc // n_z
    home = c // per
    top, tg = ids.shape
    lanes = NX * tg
    eb = n_e // NCH
    rows_ch = eb * CAP
    slots = n_e * CAP
    dense = tg * top
    rows_d = dense // NCH
    dc = 2 * dr

    def at(chip):
        return {"dp": 2 * chip + h, "mp": j}

    def remote(src, dst, ss, rs, dev):
        return pltpu.make_async_remote_copy(src_ref=src, dst_ref=dst, send_sem=ss, recv_sem=rs, device_id=dev, device_id_type=MESH)

    own_w = [pltpu.make_async_copy(a, b, loc.at[i]) for i, (a, b) in enumerate(((wg, wog), (wu, wou), (wd, wod)))]
    for cp in own_w:
        cp.start()
    for i in range(per):
        tokp[i] = tok[:, i * dc : (i + 1) * dc]

    lane_g = sum([(lax.broadcasted_iota(jnp.int32, (1, lanes), 1) >= i * tg).astype(jnp.int32) for i in range(1, NX)], jnp.zeros((1, lanes), jnp.int32))
    mine = jnp.where(lane_g == x, jnp.concatenate([ids[...]] * NX, axis=1), -1)
    ids_all[c] = mine

    barrier = pltpu.get_barrier_semaphore()

    def greet(k, _):
        pl.semaphore_signal(barrier, inc=1, device_id={"dp": (dp + k) % n_dp, "mp": j}, device_id_type=MESH)
        return 0

    lax.fori_loop(1, n_dp, greet, 0)

    def greet_z(k, _):
        pl.semaphore_signal(barrier, inc=1, device_id={"dp": dp, "mp": (j + k) % n_z}, device_id_type=MESH)
        return 0

    lax.fori_loop(1, n_z, greet_z, 0)
    for i in range(per):

        @pl.when(per * j + i != c)
        def _():
            pl.semaphore_signal(barrier, inc=1, device_id={"dp": 2 * (per * j + i) + h, "mp": home}, device_id_type=MESH)

    for cp in own_w:
        cp.wait()

    def pack(s, _):
        e = inv[s]
        to = (s // (2 * NX), (s // 2) % NX, s % 2)
        packed[to[0], to[1], to[2], 0] = wog[e]
        packed[to[0], to[1], to[2], 1] = wou[e]
        packed[to[0], to[1], to[2], 2] = wod[e]
        return 0

    lax.fori_loop(0, n_e, pack, 0)
    pl.semaphore_wait(barrier, n_dp + n_z - 2 + per - jnp.where(home == j, 1, 0))

    def t_copy(i):
        return remote(tokp.at[i], xs.at[c], t_s.at[i], t_r.at[c % per], {"dp": 2 * (per * j + i) + h, "mp": home})

    def t_from(i):
        return remote(tokp.at[i], xs.at[per * j + i], t_s.at[i], t_r.at[i], {"dp": 2 * (per * j + i) + h, "mp": home})

    for i in range(per):

        @pl.when(per * j + i != c)
        def _():
            t_copy(i).start()

    @pl.when(home == j)
    def _():
        xs[c] = tokp[c % per]

    def ids_copy(k):
        return remote(ids_all.at[c], ids_all.at[c], ids_s.at[k], ids_r.at[k], at((c + k) % nc))

    def ids_start(k, _):
        ids_copy(k).start()
        return 0

    lax.fori_loop(1, nc, ids_start, 0)
    sib_w = [
        remote(a, b, w_s.at[i], w_r.at[i], {"dp": sib, "mp": j})
        for i, (a, b) in enumerate(((wg, wsg), (wu, wsu), (wd, wsd)))
    ]
    for cp in sib_w:
        cp.start()

    hr = dr // 2
    top_rows, low_rows = pl.ds(0, hr), pl.ds(hr, hr)

    def f1_copy(k, low):
        if low:
            to = (y + k) % NY
            return remote(packed.at[to, :, :, :, low_rows, :], st_b.at[y], f1_s.at[1, k - 1], f1_r.at[1, k - 1], at(to * NX + x))
        to = (x + k) % NX
        return remote(packed.at[:, to, :, :, top_rows, :], st_a.at[x], f1_s.at[0, k - 1], f1_r.at[0, k - 1], at(y * NX + to))

    def f1_from(k, low):
        if low:
            src = (y + NY - k) % NY
            return remote(packed.at[y, :, :, :, low_rows, :], st_b.at[src], f1_s.at[1, k - 1], f1_r.at[1, k - 1], at(src * NX + x))
        src = (x + NX - k) % NX
        return remote(packed.at[:, x, :, :, top_rows, :], st_a.at[src], f1_s.at[0, k - 1], f1_r.at[0, k - 1], at(y * NX + src))

    f1_own = [
        pltpu.make_async_copy(packed.at[:, x, :, :, top_rows, :], st_a.at[x], loc.at[4]),
        pltpu.make_async_copy(packed.at[y, :, :, :, low_rows, :], st_b.at[y], loc.at[5]),
    ]

    def f2_copy(k, d, low):
        core = (h + d) % 2
        if low:
            to = (x + k) % NX
            return remote(st_b.at[:, to, core], fresh.at[:, x, h, :, low_rows, :], f2_s.at[1, k, d], f2_r.at[1, k, d], {"dp": 2 * (y * NX + to) + core, "mp": j})
        to = (y + k) % NY
        return remote(st_a.at[:, to, core], fresh.at[y, :, h, :, top_rows, :], f2_s.at[0, k, d], f2_r.at[0, k, d], {"dp": 2 * (to * NX + x) + core, "mp": j})

    def f2_from(k, d, low):
        core = (h + d) % 2
        if low:
            src = (x + NX - k) % NX
            return remote(st_b.at[:, x, h], fresh.at[:, src, core, :, low_rows, :], f2_s.at[1, k, d], f2_r.at[1, k, d], {"dp": 2 * (y * NX + src) + core, "mp": j})
        src = (y + NY - k) % NY
        return remote(st_a.at[:, y, h], fresh.at[src, :, core, :, top_rows, :], f2_s.at[0, k, d], f2_r.at[0, k, d], {"dp": 2 * (src * NX + x) + core, "mp": j})

    f2_own = [
        pltpu.make_async_copy(st_a.at[:, y, h], fresh.at[y, :, h, :, top_rows, :], loc.at[4]),
        pltpu.make_async_copy(st_b.at[:, x, h], fresh.at[:, x, h, :, low_rows, :], loc.at[5]),
    ]
    steps = [(k, d) for k in range(max(NX, NY)) for d in range(2) if k or d]

    def f2_start(ks):
        for k, d in steps:
            if k in ks:
                if k < NY:
                    f2_copy(k, d, False).start()
                if k < NX:
                    f2_copy(k, d, True).start()

    for cp in f1_own:
        cp.start()
    for k in range(1, NX):
        f1_copy(k, False).start()
    for k in range(1, NY):
        f1_copy(k, True).start()

    lane_i = lax.broadcasted_iota(jnp.int32, (lanes, lanes), 1)
    row_i = lax.broadcasted_iota(jnp.int32, (lanes, lanes), 0)
    lane_of = sum([(lane_i >= i * tg).astype(jnp.int32) for i in range(1, NX)], jnp.zeros((lanes, lanes), jnp.int32))
    row_of = sum([(row_i >= i * tg).astype(jnp.int32) for i in range(1, NX)], jnp.zeros((lanes, lanes), jnp.int32))
    before = jnp.where((row_i < lane_i) & (lane_of == row_of), 1.0, 0.0).astype(BF16)
    e_iota = lax.broadcasted_iota(jnp.int32, (n_e, lanes), 0)
    rw4 = jnp.concatenate([rw[...]] * NX, axis=1)

    def positions(ids):
        named = jnp.zeros((n_e, lanes), F32)
        for i in range(top):
            named = jnp.where(ids[i : i + 1, :] == e_iota, 1.0, named)
        count = jnp.dot(named.astype(BF16), before, preferred_element_type=F32)
        return jnp.where(named > 0.5, count, -1.0)

    my_pos = positions(mine)
    my_w = jnp.zeros((n_e, lanes), F32)
    for i in range(top):
        my_w = jnp.where(mine[i : i + 1, :] == e_iota, rw4[i : i + 1, :], my_w)
    e_row = lax.broadcasted_iota(jnp.int32, (n_e, n_e), 0)
    e_col = lax.broadcasted_iota(jnp.int32, (n_e, n_e), 1)
    below = jnp.where(e_col < e_row, 1.0, 0.0).astype(BF16)
    d_iota = lax.broadcasted_iota(jnp.int32, (n_e, rows_d), 1).astype(F32)
    p_dense = lax.broadcasted_iota(jnp.int32, (CAP, rows_d), 0).astype(F32)

    def dense_places(named):
        count = jnp.broadcast_to(jnp.sum(named, axis=1, keepdims=True), (n_e, rows_d))
        start = jnp.dot(below, count.astype(BF16), preferred_element_type=F32)
        out = []
        for m in range(NCH):
            at_row = d_iota + float(m * rows_d) - start
            out.append(jnp.where((at_row >= 0.0) & (at_row < count), at_row, -1.0))
        return out

    def spots(held):
        n = held.shape[0]
        hot = jnp.where(held.reshape(n, 1, rows_d) == p_dense[None], 1.0, 0.0)
        return hot.reshape(n * CAP, rows_d)

    my_named = jnp.where(my_pos >= 0.0, 1.0, 0.0)
    my_places = dense_places(my_named)
    p_iota = lax.broadcasted_iota(jnp.int32, (CAP, lanes), 0).astype(F32)
    slot_w = []
    for q in range(NCH):
        pe = my_pos[q * eb : (q + 1) * eb, :].reshape(eb, 1, lanes)
        we = my_w[q * eb : (q + 1) * eb, :].reshape(eb, 1, lanes)
        ws = jnp.sum(jnp.where(pe == p_iota[None], we, 0.0), axis=2, keepdims=True)
        slot_w.append(jnp.broadcast_to(ws.reshape(rows_ch, 1), (rows_ch, BLK)))
    for m in range(NCH):
        acc = jnp.zeros((rows_d, BLK), F32)
        for q in range(max(0, m - 1), min(NCH, m + 2)):
            hot = spots(my_places[m][q * eb : (q + 1) * eb, :])
            acc = acc + lax.dot_general(hot, slot_w[q], (((0,), (0,)), ((), ())), preferred_element_type=F32, precision=lax.Precision.HIGHEST)
        row_w[m * rows_d : (m + 1) * rows_d, :] = acc

    far = n_z // 2
    hp = per // 2

    def z_copy(s, way):
        src = (j + n_z - s) % n_z if way == 0 else (j + s) % n_z
        to = (j + 1) % n_z if way == 0 else (j + n_z - 1) % n_z
        held = xs.at[pl.ds(per * src + way * hp, hp)] if s == far - 1 else xs.at[pl.ds(per * src, per)]
        return remote(held, held, z_s.at[way, s], z_r.at[way, s], {"dp": dp, "mp": to})

    def z_from(s, way):
        src = (j + n_z - s - 1) % n_z if way == 0 else (j + s + 1) % n_z
        to = (j + n_z - 1) % n_z if way == 0 else (j + 1) % n_z
        held = xs.at[pl.ds(per * src + way * hp, hp)] if s == far - 1 else xs.at[pl.ds(per * src, per)]
        return remote(held, held, z_s.at[way, s], z_r.at[way, s], {"dp": dp, "mp": to})

    for i in range(per):

        @pl.when(per * j + i != c)
        def _():
            t_from(i).wait_recv()

    for way in range(2):
        z_copy(0, way).start()

    def ids_wait(k, _):
        src = (c + nc - k) % nc
        remote(ids_all.at[src], ids_all.at[src], ids_s.at[k], ids_r.at[k], at(src)).wait_recv()
        return 0

    lax.fori_loop(1, nc, ids_wait, 0)

    r_iota = lax.broadcasted_iota(jnp.int32, (NX * CAP, lanes), 0)
    r_of = sum([(r_iota >= i * CAP).astype(jnp.int32) for i in range(1, NX)], jnp.zeros((NX * CAP, lanes), jnp.int32))
    want = jnp.where(r_of == lane_g, r_iota - CAP * r_of, -9).astype(F32)

    def place(b, _):
        ids = ids_all[b * NX]
        for i in range(1, NX):
            ids = jnp.maximum(ids, ids_all[b * NX + i])
        pos = positions(ids)
        for i in range(NX):
            held = dense_places(jnp.where((pos >= 0.0) & (lane_g == i), 1.0, 0.0))
            for m in range(NCH):
                places[b * NX + i, m] = held[m]

        for q in range(NCH):
            pe = pos[q * eb : (q + 1) * eb, :].reshape(eb, 1, lanes)
            hots[b, q] = jnp.where(pe == want[None], 1.0, 0.0).astype(BF16).reshape(eb * NX * CAP, lanes)
        return 0

    for s in range(1, far):
        lax.fori_loop(NY * (s - 1) // (far - 1), NY * s // (far - 1), place, 0)
        for way in range(2):
            z_from(s - 1, way).wait_recv()
            z_copy(s, way).start()
    for way in range(2):
        z_from(far - 1, way).wait_recv()
    for cp in sib_w:
        cp.wait_recv()


    def pick(q, b):
        tokens = xs[pl.ds(b * NX, NX)].reshape(lanes, dc)
        he = eb // 2
        for i in range(2):
            got = jnp.dot(hots[b, q, pl.ds(i * he * NX * CAP, he * NX * CAP), :], tokens, preferred_element_type=F32)
            xg[pl.ds(q * eb + i * he, he), b] = got.astype(BF16).reshape(he, NX * CAP, dc)

    def by_core(own, other):
        return jnp.concatenate([jnp.where(h == 0, own, other), jnp.where(h == 0, other, own)], axis=0)

    def project(e):
        a = xg[e].reshape(NY * NX * CAP, dc)
        w = jnp.concatenate([by_core(wog[e], wsg[e]), by_core(wou[e], wsu[e])], axis=1)
        return jnp.dot(a, w, preferred_element_type=F32).reshape(nc, CAP, 2 * BLK)

    def slots_of(q):
        return pl.ds(pl.multiple_of(q * rows_ch, rows_ch), rows_ch)

    def rows_of(q):
        return pl.ds(pl.multiple_of(q * rows_d, rows_d), rows_d)

    def with_near(q, work):
        @pl.when(q == 0)
        def _():
            work(0, 2)

        @pl.when((q > 0) & (q < NCH - 1))
        def _():
            work(q - 1, 3)

        @pl.when(q == NCH - 1)
        def _():
            work(NCH - 2, 2)

    hy, hx = NY // 2, NX // 2

    def near(way, up):
        if up:
            return (y + 1) % NY if way == 0 else (y + NY - 1) % NY
        return (x + 1) % NX if way == 0 else (x + NX - 1) % NX

    def chip_near(way, up):
        return near(way, up) * NX + x if up else y * NX + near(way, up)

    def r0_copy(q, way, up):
        if up:
            src, dst = dens.at[(y + 2) % NY, pl.ds(way * hx, hx), rows_of(q), pl.ds(BLK, BLK)], hu
        else:
            src, dst = dens.at[pl.ds(way * hy, hy), (x + 2) % NX, rows_of(q), pl.ds(0, BLK)], hg
        u = int(up)
        return remote(src, dst.at[way, :, rows_of(q), :], r0_s.at[u, q, way], r0_r.at[u, q, way], at(chip_near(way, up)))

    def r1_copy(q, way, up):
        if up:
            src, dst = dens.at[near(way, up), :, rows_of(q), pl.ds(BLK, BLK)], ru
        else:
            src, dst = dens.at[:, near(way, up), rows_of(q), pl.ds(0, BLK)], rg
        u = int(up)
        return remote(src, dst.at[way, :, rows_of(q), :], r1_s.at[u, q, way], r1_r.at[u, q, way], at(chip_near(way, up)))

    def pass_on(q):
        rows = rows_of(q)
        for way in range(2):
            r0_copy(q, way, False).wait_recv()
            half_y = pl.ds(way * hy, hy)
            got = dens[half_y, near(way, False), rows, pl.ds(0, BLK)].astype(F32) + hg[way, :, rows, :].astype(F32)
            dens[half_y, near(way, False), rows, pl.ds(0, BLK)] = got.astype(BF16)
            r1_copy(q, way, False).start()
            r0_copy(q, way, True).wait_recv()
            half_x = pl.ds(way * hx, hx)
            got = dens[near(way, True), half_x, rows, pl.ds(BLK, BLK)].astype(F32) + hu[way, :, rows, :].astype(F32)
            dens[near(way, True), half_x, rows, pl.ds(BLK, BLK)] = got.astype(BF16)
            r1_copy(q, way, True).start()

    def first(q):
        for b in range(NY):
            pick(q, b)

        def pair(i, _):
            e = q * eb + 2 * i
            both = jnp.concatenate([project(e), project(e + 1)], axis=1).astype(BF16)
            part[:, :, pl.ds(pl.multiple_of(e * CAP, 2 * CAP), 2 * CAP), :] = both.reshape(NY, NX, 2 * CAP, 2 * BLK)
            return 0

        lax.fori_loop(0, eb // 2, pair, 0)
    def compact(m):
        def work(w, n):
            experts = pl.ds(pl.multiple_of(w * eb, eb), n * eb)
            near_slots = pl.ds(pl.multiple_of(w * rows_ch, rows_ch), n * rows_ch)

            def one(b, _):
                got = []
                for i in range(NX):
                    hot = spots(places[b * NX + i, m, experts, :]).astype(BF16)
                    got.append(lax.dot_general(hot, part[b, i, near_slots, :], (((0,), (0,)), ((), ())), preferred_element_type=F32))
                for i in range(NX):
                    dens[b, i, rows_of(m), :] = got[i].astype(BF16)
                return 0

            lax.fori_loop(0, NY, one, 0)

        with_near(m, work)
        for way in range(2):
            r0_copy(m, way, False).start()
            r0_copy(m, way, True).start()

    def r2_copy(q, k, up):
        if up:
            to = (x + k) % NX
            return remote(dens.at[y, to, rows_of(q), pl.ds(BLK, BLK)], r2u.at[k - 1, rows_of(q), :], r2_s.at[1, q, k - 1], r2_r.at[1, q, k - 1], at(y * NX + to))
        to = (y + k) % NY
        return remote(dens.at[to, x, rows_of(q), pl.ds(0, BLK)], r2g.at[k - 1, rows_of(q), :], r2_s.at[0, q, k - 1], r2_r.at[0, q, k - 1], at(to * NX + x))

    def second(q):
        rows = rows_of(q)
        for way in range(2):
            r1_copy(q, way, False).wait_recv()

        def sum_g(i, _):
            t = dens[i, x, rows, pl.ds(0, BLK)].astype(F32)
            for way in range(2):
                t = t + rg[way, i, rows, :].astype(F32)
            dens[i, x, rows, pl.ds(0, BLK)] = t.astype(BF16)
            return 0

        lax.fori_loop(0, NY, sum_g, 0)
        for k in range(1, NY):
            r2_copy(q, k, False).start()
        for way in range(2):
            r1_copy(q, way, True).wait_recv()

        def sum_u(i, _):
            t = dens[y, i, rows, pl.ds(BLK, BLK)].astype(F32)
            for way in range(2):
                t = t + ru[way, i, rows, :].astype(F32)
            dens[y, i, rows, pl.ds(BLK, BLK)] = t.astype(BF16)
            return 0

        lax.fori_loop(0, NX, sum_u, 0)
        for k in range(1, NX):
            r2_copy(q, k, True).start()
        return 0


    def line(q_along_x, k):
        if q_along_x:
            return y * NX + (x + k) % NX
        return ((y + k) % NY) * NX + x

    hr_ch = rows_d // 2

    def half_of(q, along_x, part_of=None):
        start, size = q * rows_d + (0 if along_x else hr_ch), hr_ch
        if part_of is not None:
            start, size = start + part_of * (hr_ch // 2), hr_ch // 2
        return pl.ds(pl.multiple_of(start, hr_ch // 2), size)

    def a1_copy(q, k, along_x):
        sl = hid.at[y, x, half_of(q, along_x), :]
        u = int(along_x)
        return remote(sl, sl, a1_s.at[u, q, k], a1_r.at[u, q, k], at(line(along_x, k)))

    def a1_from(q, k, along_x):
        src = line(along_x, (NX if along_x else NY) - k)
        sl = hid.at[src // NX, src % NX, half_of(q, along_x), :]
        u = int(along_x)
        return remote(sl, sl, a1_s.at[u, q, k], a1_r.at[u, q, k], at(src))

    def row_block(along_x, place, rows):
        return hid.at[place, :, rows, :] if along_x else hid.at[:, place, rows, :]

    def a2_copy(q, way, along_x):
        sl = row_block(along_x, y if along_x else x, half_of(q, along_x))
        u = int(along_x)
        return remote(sl, sl, a2_s.at[u, q, way], a2_r.at[u, q, way], at(chip_near(way, along_x)))

    def a2_from(q, way, along_x):
        sl = row_block(along_x, near(1 - way, along_x), half_of(q, along_x))
        u = int(along_x)
        return remote(sl, sl, a2_s.at[u, q, way], a2_r.at[u, q, way], at(chip_near(1 - way, along_x)))

    def a3_copy(q, way, along_x):
        sl = row_block(along_x, near(1 - way, along_x), half_of(q, along_x, way))
        u = int(along_x)
        return remote(sl, sl, a3_s.at[u, q, way], a3_r.at[u, q, way], at(chip_near(way, along_x)))

    def a3_from(q, way, along_x):
        sl = row_block(along_x, (y + 2) % NY if along_x else (x + 2) % NX, half_of(q, along_x, way))
        u = int(along_x)
        return remote(sl, sl, a3_s.at[u, q, way], a3_r.at[u, q, way], at(chip_near(1 - way, along_x)))

    def third(q):
        rows = rows_of(q)
        for k in range(1, NY):
            r2_copy(q, k, False).wait_recv()
        for k in range(1, NX):
            r2_copy(q, k, True).wait_recv()
        gate = dens[y, x, rows, pl.ds(0, BLK)].astype(F32)
        for k in range(NY - 1):
            gate = gate + r2g[k, rows, :].astype(F32)
        up = dens[y, x, rows, pl.ds(BLK, BLK)].astype(F32)
        for k in range(NX - 1):
            up = up + r2u[k, rows, :].astype(F32)
        value = gate / (1.0 + jnp.exp(-gate)) * up * row_w[rows, :]
        hid[y, x, rows, :] = value.astype(BF16)
        for k in range(1, NX):
            a1_copy(q, k, True).start()
        for k in range(1, NY):
            a1_copy(q, k, False).start()

    def spread(q):
        for along_x in (True, False):
            for k in range(1, NX if along_x else NY):
                a1_from(q, k, along_x).wait_recv()
            for way in range(2):
                a2_copy(q, way, along_x).start()

    def forward(q):
        for along_x in (True, False):
            for way in range(2):
                a2_from(q, way, along_x).wait_recv()
                a3_copy(q, way, along_x).start()

    def arrive(q):
        for along_x in (True, False):
            for way in range(2):
                a3_from(q, way, along_x).wait_recv()

    def down(q):
        experts = pl.ds(pl.multiple_of(q * eb, eb), eb)

        def work(w, n):
            near_rows = pl.ds(pl.multiple_of(w * rows_d, rows_d), n * rows_d)

            def one(b, _):
                got = []
                for i in range(NX):
                    hot = jnp.concatenate([spots(places[b * NX + i, w + d, experts, :]) for d in range(n)], axis=1).astype(BF16)
                    got.append(jnp.dot(hot, hid[b, i, near_rows, :], preferred_element_type=F32))
                for i in range(NX):
                    part[b, i, slots_of(q), pl.ds(0, BLK)] = got[i].astype(BF16)
                return 0

            lax.fori_loop(0, NY, one, 0)

        with_near(q, work)

        def pair(i, _):
            e = q * eb + 2 * i
            both = part[:, :, pl.ds(pl.multiple_of(e * CAP, 2 * CAP), 2 * CAP), pl.ds(0, BLK)].astype(F32).reshape(nc, 2 * CAP, BLK)
            for o in range(2):
                a = both[:, o * CAP : (o + 1) * CAP, :].reshape(nc * CAP, BLK).astype(BF16)
                w = by_core(wod[e + o], wsd[e + o])
                got = lax.dot_general(a, w, (((1,), (1,)), ((), ())), preferred_element_type=F32)
                xg[e + o] = got.astype(BF16).reshape(NY, NX * CAP, dc)
            return 0

        lax.fori_loop(0, eb // 2, pair, 0)

    stages = [first, compact]
    stages += [pass_on, second]
    stages += [third]
    stages += [spread, forward, arrive, down]

    def beat(t, _):
        for n, stage in enumerate(stages):

            @pl.when((t >= n) & (t < n + NCH))
            def _():
                stage(t - n)

        @pl.when(t == REST)
        def _():
            for cp in f1_own:
                cp.wait()
            for k in range(1, NX):
                f1_from(k, False).wait_recv()
            for k in range(1, NY):
                f1_from(k, True).wait_recv()
            for cp in f2_own:
                cp.start()
            f2_start(range(max(NX, NY)))

        return 0

    lax.fori_loop(0, NCH + len(stages) - 1, beat, 0)
    for s in range(far):
        for way in range(2):
            z_copy(s, way).wait_send()
    outp = xs

    per_row = NX // per

    def zo_copy(to, n):
        k = (to + n_z - j) % n_z
        return remote(outp.at[per * to + n], zb.at[n, k], zo_s.at[n, k], zo_r.at[n, k], {"dp": dp, "mp": to})

    def from_z(k, n):
        src = (j + n_z - k) % n_z
        return remote(outp.at[per * src + n], zb.at[n, k], zo_s.at[n, k], zo_r.at[n, k], {"dp": dp, "mp": src})

    def combine(i, _):
        b = (j // per_row + 1 + i) % NY
        total = jnp.zeros((lanes, dc), F32)
        for q in range(NCH):
            d = xg[pl.ds(q * eb, eb), b].reshape(eb * NX * CAP, dc)
            total = total + lax.dot_general(hots[b, q], d, (((0,), (0,)), ((), ())), preferred_element_type=F32)
        outp[pl.ds(b * NX, NX)] = total.astype(BF16).reshape(NX, tg, dc)
        for n in range(per_row):
            to = b * per_row + n

            @pl.when(to != j)
            def _():
                zo_copy(to, 0).start()

        return 0

    lax.fori_loop(0, NY, combine, 0)
    def zo_start(k, _):
        for n in range(1, per):
            zo_copy((j + k) % n_z, n).start()
        return 0

    lax.fori_loop(1, n_z, zo_start, 0)

    def m_copy(i):
        return remote(fin.at[i], ob.at[c % per], m_s.at[i], m_r.at[c % per], {"dp": 2 * (per * j + i) + h, "mp": home})

    def m_from(i):
        return remote(fin.at[i], ob.at[i], m_s.at[i], m_r.at[i], {"dp": 2 * (per * j + i) + h, "mp": home})

    for i in range(per):
        total = outp[per * j + i].astype(F32)
        for k in range(1, n_z):
            from_z(k, i).wait_recv()
            total = total + zb[i, k].astype(F32)
        fin[i] = total.astype(BF16)

        @pl.when(per * j + i != c)
        def _():
            m_copy(i).start()

    @pl.when(home == j)
    def _():
        ob[c % per] = fin[c % per]

    for i in range(per):

        @pl.when(per * j + i != c)
        def _():
            m_from(i).wait_recv()

    mix[...] = jnp.concatenate([ob[i] for i in range(per)], axis=1)

    for cp in f2_own:
        cp.wait()
    for k, d in steps:
        if k < NY:
            f2_from(k, d, False).wait_recv()
            f2_copy(k, d, False).wait_send()
        if k < NX:
            f2_from(k, d, True).wait_recv()
            f2_copy(k, d, True).wait_send()
    for k in range(1, NX):
        f1_copy(k, False).wait_send()
    for k in range(1, NY):
        f1_copy(k, True).wait_send()
    def z_done(k, _):
        for n in range(per):
            zo_copy((j + k) % n_z, n).wait_send()
        return 0

    lax.fori_loop(1, n_z, z_done, 0)
    for i in range(per):

        @pl.when(per * j + i != c)
        def _():
            t_copy(i).wait_send()
            m_copy(i).wait_send()

    def plane_done(k, _):
        ids_copy(k).wait_send()
        return 0

    lax.fori_loop(1, nc, plane_done, 0)
    for cp in sib_w:
        cp.wait_send()

    def sums_done(q, _):
        for way in range(2):
            for up in (False, True):
                r0_copy(q, way, up).wait_send()
                r1_copy(q, way, up).wait_send()
        for k in range(1, NX):
            r2_copy(q, k, True).wait_send()
        for k in range(1, NY):
            r2_copy(q, k, False).wait_send()
        return 0

    lax.fori_loop(0, NCH, sums_done, 0)

    def hid_done(q, _):
        for along_x in (True, False):
            for k in range(1, NX if along_x else NY):
                a1_copy(q, k, along_x).wait_send()
            for way in range(2):
                a2_copy(q, way, along_x).wait_send()
                a3_copy(q, way, along_x).wait_send()
        return 0

    lax.fori_loop(0, NCH, hid_done, 0)


def quantize_kernel(fresh, gate, up, down, scales):
    rows = gate.shape[1]
    for m, out in enumerate((gate, up, down)):
        w = fresh[:, m].reshape(rows // BLK, BLK, BLK).astype(F32)
        top = jnp.max(jnp.max(jnp.abs(w), axis=1, keepdims=True), axis=2, keepdims=True) + EPS
        out[0] = (w * (1.0 / top)).astype(BF16).reshape(rows, BLK)
        scales[m, 0] = top.reshape(rows // BLK, 1)


def local(tokens, expert_ids, route_weights, placement_of, gate_weight, up_weight, down_weight):
    n_dp, n_z = lax.axis_size("dp"), lax.axis_size("mp")
    nc = n_dp // 2
    n_e, dr, _ = gate_weight.shape
    tg, wide = tokens.shape
    top = expert_ids.shape[1]
    dc, per, lanes = 2 * dr, wide // (2 * dr), NX * tg
    slots = n_e * CAP

    order = jnp.arange(n_e, dtype=jnp.int32)
    inv = jnp.sum(jnp.where(placement_of[:, None] == order[None, :], order[:, None], 0), axis=0)

    vm = pltpu.VMEM
    dma = pltpu.SemaphoreType.DMA
    hbm = pl.BlockSpec(memory_space=pl.ANY)
    vmem = pl.BlockSpec(memory_space=pltpu.VMEM)
    weights = [vm((n_e, dr, BLK), BF16)] * 6
    fresh, mix = pl.pallas_call(
        routed_kernel,
        out_shape=(
            jax.ShapeDtypeStruct((NY, NX, 2, 3, dr, BLK), BF16),
            jax.ShapeDtypeStruct((tg, wide), BF16),
        ),
        in_specs=[pl.BlockSpec(memory_space=pltpu.SMEM), vmem, vmem, vmem, hbm, hbm, hbm],
        out_specs=(hbm, vmem),
        scratch_shapes=weights
        + [
            vm((NY, NX, 2, 3, dr, BLK), BF16),
            vm((NX, NY, 2, 3, dr // 2, BLK), BF16),
            vm((NY, NX, 2, 3, dr // 2, BLK), BF16),
            vm((per, tg, dc), BF16),
            vm((nc, top, lanes), jnp.int32),
            vm((NY, NCH, slots // NCH * NX, lanes), BF16),
            vm((nc, NCH, n_e, tg * top // NCH), F32),
            vm((tg * top, BLK), F32),
            vm((nc, tg, dc), BF16),
            vm((n_e, NY, NX * CAP, dc), BF16),
            vm((NY, NX, slots, 2 * BLK), BF16),
            vm((NY, NX, tg * top, 2 * BLK), BF16),
            vm((2, NY // 2, tg * top, BLK), BF16),
            vm((2, NX // 2, tg * top, BLK), BF16),
            vm((2, NY, tg * top, BLK), BF16),
            vm((2, NX, tg * top, BLK), BF16),
            vm((NY - 1, tg * top, BLK), BF16),
            vm((NX - 1, tg * top, BLK), BF16),
            vm((NY, NX, tg * top, BLK), BF16),
            vm((per, n_z, tg, dc), BF16),
            vm((per, tg, dc), BF16),
            vm((per, tg, dc), BF16),
            dma((6,)),
            dma((nc,)), dma((nc,)),
            dma((2, n_z // 2)), dma((2, n_z // 2)),
            dma((per,)), dma((per,)),
            dma((3,)), dma((3,)),
            dma((2, NCH, 2)), dma((2, NCH, 2)),
            dma((2, NCH, 2)), dma((2, NCH, 2)),
            dma((2, NCH, 3)), dma((2, NCH, 3)),
            dma((2, NCH, 4)), dma((2, NCH, 4)),
            dma((2, NCH, 2)), dma((2, NCH, 2)),
            dma((2, NCH, 2)), dma((2, NCH, 2)),
            dma((per, n_z)), dma((per, n_z)),
            dma((per,)), dma((per,)),
            dma((2, 3)), dma((2, 3)),
            dma((2, 4, 2)), dma((2, 4, 2)),
        ],
        compiler_params=pltpu.CompilerParams(collective_id=0, has_side_effects=True, vmem_limit_bytes=63 * 1024 * 1024),
    )(inv, expert_ids.T, route_weights.T, tokens, gate_weight, up_weight, down_weight)
    fresh = fresh.reshape(n_dp, 3, dr, BLK)

    step = n_dp // 2
    rows = step * dr
    grid = n_dp // step
    out_w = jax.ShapeDtypeStruct((1, n_dp * dr, BLK), BF16)
    spec_w = pl.BlockSpec((1, rows, BLK), lambda i: (0, i, 0))
    gate_q, up_q, down_q, scales = pl.pallas_call(
        quantize_kernel,
        grid=(grid,),
        out_shape=(out_w, out_w, out_w, jax.ShapeDtypeStruct((3, grid, rows // BLK, 1), F32)),
        in_specs=[pl.BlockSpec((step, 3, dr, BLK), lambda i: (i, 0, 0, 0))],
        out_specs=(spec_w, spec_w, spec_w, pl.BlockSpec((3, 1, rows // BLK, 1), lambda i: (0, i, 0, 0))),
        compiler_params=pltpu.CompilerParams(vmem_limit_bytes=48 * 1024 * 1024),
    )(fresh)
    scales = scales.reshape(3, 1, -1, 1)

    return gate_q, up_q, down_q, scales, mix


def solution(mesh):
    placed = (
        P("dp", "mp"),
        P("dp", None),
        P("dp", None),
        P(),
        P(None, "dp", "mp"),
        P(None, "dp", "mp"),
        P(None, "dp", "mp"),
    )
    return jax.shard_map(
        local,
        mesh=mesh,
        in_specs=placed,
        out_specs=(
            P("dp", None, "mp"),
            P("dp", None, "mp"),
            P("dp", None, "mp"),
            P(None, "dp", None, "mp"),
            P("dp", "mp"),
        ),
        check_vma=False,
    )
```

```python
import jax
import jax.numpy as jnp
from jax import lax
from jax.experimental import pallas as pl
from jax.experimental.pallas import tpu as pltpu
from jax.sharding import PartitionSpec as P

BLK = 128
CAP = 24
EPS = 1e-06
NY, NX = 4, 4
NCH = 4
REST = NCH + 6
MESH = pl.DeviceIdType.MESH
F32, BF16 = jnp.float32, jnp.bfloat16


def routed_kernel(
    placement, ids, rw, tok, wg, wu, wd,
    fresh, mix,
    inv, wog, wou, wod, wsg, wsu, wsd, packed, st_a, st_b, tokp, ids_all, hots, places, row_w, xs, xg, part, dens,
    hg, hu, rg, ru, r2g, r2u, hid, zb, fin, ob,
    loc, ids_s, ids_r, z_s, z_r, t_s, t_r, w_s, w_r, r0_s, r0_r, r1_s, r1_r, r2_s, r2_r,
    a1_s, a1_r, a2_s, a2_r, a3_s, a3_r, zo_s, zo_r, m_s, m_r, f1_s, f1_r, f2_s, f2_r,
):
    dp, j = lax.axis_index("dp"), lax.axis_index("mp")
    n_dp, n_z = lax.axis_size("dp"), lax.axis_size("mp")
    nc = NX * NY
    c, h = dp // 2, dp % 2
    y, x = c // NX, c % NX
    sib = 2 * c + 1 - h
    n_e, dr, _ = wog.shape
    per = nc // n_z
    home = c // per
    top, tg = ids.shape
    lanes = NX * tg
    eb = n_e // NCH
    rows_ch = eb * CAP
    slots = n_e * CAP
    dense = tg * top
    rows_d = dense // NCH
    dc = 2 * dr

    def at(chip):
        return {"dp": 2 * chip + h, "mp": j}

    def remote(src, dst, ss, rs, dev):
        return pltpu.make_async_remote_copy(src_ref=src, dst_ref=dst, send_sem=ss, recv_sem=rs, device_id=dev, device_id_type=MESH)

    own_w = [pltpu.make_async_copy(a, b, loc.at[i]) for i, (a, b) in enumerate(((wg, wog), (wu, wou), (wd, wod)))]
    for cp in own_w:
        cp.start()
    for i in range(per):
        tokp[i] = tok[:, i * dc : (i + 1) * dc]

    lane_g = sum([(lax.broadcasted_iota(jnp.int32, (1, lanes), 1) >= i * tg).astype(jnp.int32) for i in range(1, NX)], jnp.zeros((1, lanes), jnp.int32))
    mine = jnp.where(lane_g == x, jnp.concatenate([ids[...]] * NX, axis=1), -1)
    ids_all[c] = mine

    barrier = pltpu.get_barrier_semaphore()

    def greet(k, _):
        pl.semaphore_signal(barrier, inc=1, device_id={"dp": (dp + k) % n_dp, "mp": j}, device_id_type=MESH)
        return 0

    lax.fori_loop(1, n_dp, greet, 0)

    def greet_z(k, _):
        pl.semaphore_signal(barrier, inc=1, device_id={"dp": dp, "mp": (j + k) % n_z}, device_id_type=MESH)
        return 0

    lax.fori_loop(1, n_z, greet_z, 0)
    for i in range(per):

        @pl.when(per * j + i != c)
        def _():
            pl.semaphore_signal(barrier, inc=1, device_id={"dp": 2 * (per * j + i) + h, "mp": home}, device_id_type=MESH)

    def find(s, _):
        e = jnp.int32(0)
        for i in range(n_e):
            e = jnp.maximum(e, jnp.where(placement[i] == s, jnp.int32(i), jnp.int32(0)))
        inv[s] = e
        return 0

    lax.fori_loop(0, n_e, find, 0)
    for cp in own_w:
        cp.wait()

    def pack(s, _):
        e = inv[s]
        to = (s // (2 * NX), (s // 2) % NX, s % 2)
        packed[to[0], to[1], to[2], 0] = wog[e]
        packed[to[0], to[1], to[2], 1] = wou[e]
        packed[to[0], to[1], to[2], 2] = wod[e]
        return 0

    lax.fori_loop(0, n_e, pack, 0)
    pl.semaphore_wait(barrier, n_dp + n_z - 2 + per - jnp.where(home == j, 1, 0))

    def t_copy(i):
        return remote(tokp.at[i], xs.at[c], t_s.at[i], t_r.at[c % per], {"dp": 2 * (per * j + i) + h, "mp": home})

    def t_from(i):
        return remote(tokp.at[i], xs.at[per * j + i], t_s.at[i], t_r.at[i], {"dp": 2 * (per * j + i) + h, "mp": home})

    for i in range(per):

        @pl.when(per * j + i != c)
        def _():
            t_copy(i).start()

    @pl.when(home == j)
    def _():
        xs[c] = tokp[c % per]

    def ids_copy(k):
        return remote(ids_all.at[c], ids_all.at[c], ids_s.at[k], ids_r.at[k], at((c + k) % nc))

    def ids_start(k, _):
        ids_copy(k).start()
        return 0

    lax.fori_loop(1, nc, ids_start, 0)
    sib_w = [
        remote(a, b, w_s.at[i], w_r.at[i], {"dp": sib, "mp": j})
        for i, (a, b) in enumerate(((wg, wsg), (wu, wsu), (wd, wsd)))
    ]
    for cp in sib_w:
        cp.start()

    hr = dr // 2
    top_rows, low_rows = pl.ds(0, hr), pl.ds(hr, hr)

    def f1_copy(k, low):
        if low:
            to = (y + k) % NY
            return remote(packed.at[to, :, :, :, low_rows, :], st_b.at[y], f1_s.at[1, k - 1], f1_r.at[1, k - 1], at(to * NX + x))
        to = (x + k) % NX
        return remote(packed.at[:, to, :, :, top_rows, :], st_a.at[x], f1_s.at[0, k - 1], f1_r.at[0, k - 1], at(y * NX + to))

    def f1_from(k, low):
        if low:
            src = (y + NY - k) % NY
            return remote(packed.at[y, :, :, :, low_rows, :], st_b.at[src], f1_s.at[1, k - 1], f1_r.at[1, k - 1], at(src * NX + x))
        src = (x + NX - k) % NX
        return remote(packed.at[:, x, :, :, top_rows, :], st_a.at[src], f1_s.at[0, k - 1], f1_r.at[0, k - 1], at(y * NX + src))

    f1_own = [
        pltpu.make_async_copy(packed.at[:, x, :, :, top_rows, :], st_a.at[x], loc.at[4]),
        pltpu.make_async_copy(packed.at[y, :, :, :, low_rows, :], st_b.at[y], loc.at[5]),
    ]

    def f2_copy(k, d, low):
        core = (h + d) % 2
        if low:
            to = (x + k) % NX
            return remote(st_b.at[:, to, core], fresh.at[:, x, h, :, low_rows, :], f2_s.at[1, k, d], f2_r.at[1, k, d], {"dp": 2 * (y * NX + to) + core, "mp": j})
        to = (y + k) % NY
        return remote(st_a.at[:, to, core], fresh.at[y, :, h, :, top_rows, :], f2_s.at[0, k, d], f2_r.at[0, k, d], {"dp": 2 * (to * NX + x) + core, "mp": j})

    def f2_from(k, d, low):
        core = (h + d) % 2
        if low:
            src = (x + NX - k) % NX
            return remote(st_b.at[:, x, h], fresh.at[:, src, core, :, low_rows, :], f2_s.at[1, k, d], f2_r.at[1, k, d], {"dp": 2 * (y * NX + src) + core, "mp": j})
        src = (y + NY - k) % NY
        return remote(st_a.at[:, y, h], fresh.at[src, :, core, :, top_rows, :], f2_s.at[0, k, d], f2_r.at[0, k, d], {"dp": 2 * (src * NX + x) + core, "mp": j})

    f2_own = [
        pltpu.make_async_copy(st_a.at[:, y, h], fresh.at[y, :, h, :, top_rows, :], loc.at[4]),
        pltpu.make_async_copy(st_b.at[:, x, h], fresh.at[:, x, h, :, low_rows, :], loc.at[5]),
    ]
    steps = [(k, d) for k in range(max(NX, NY)) for d in range(2) if k or d]

    def f2_start(ks):
        for k, d in steps:
            if k in ks:
                if k < NY:
                    f2_copy(k, d, False).start()
                if k < NX:
                    f2_copy(k, d, True).start()

    for cp in f1_own:
        cp.start()
    for k in range(1, NX):
        f1_copy(k, False).start()
    for k in range(1, NY):
        f1_copy(k, True).start()

    lane_i = lax.broadcasted_iota(jnp.int32, (lanes, lanes), 1)
    row_i = lax.broadcasted_iota(jnp.int32, (lanes, lanes), 0)
    lane_of = sum([(lane_i >= i * tg).astype(jnp.int32) for i in range(1, NX)], jnp.zeros((lanes, lanes), jnp.int32))
    row_of = sum([(row_i >= i * tg).astype(jnp.int32) for i in range(1, NX)], jnp.zeros((lanes, lanes), jnp.int32))
    before = jnp.where((row_i < lane_i) & (lane_of == row_of), 1.0, 0.0).astype(BF16)
    e_iota = lax.broadcasted_iota(jnp.int32, (n_e, lanes), 0)
    rw4 = jnp.concatenate([rw[...]] * NX, axis=1)

    def positions(ids):
        named = jnp.zeros((n_e, lanes), F32)
        for i in range(top):
            named = jnp.where(ids[i : i + 1, :] == e_iota, 1.0, named)
        count = jnp.dot(named.astype(BF16), before, preferred_element_type=F32)
        return jnp.where(named > 0.5, count, -1.0)

    my_pos = positions(mine)
    my_w = jnp.zeros((n_e, lanes), F32)
    for i in range(top):
        my_w = jnp.where(mine[i : i + 1, :] == e_iota, rw4[i : i + 1, :], my_w)
    e_row = lax.broadcasted_iota(jnp.int32, (n_e, n_e), 0)
    e_col = lax.broadcasted_iota(jnp.int32, (n_e, n_e), 1)
    below = jnp.where(e_col < e_row, 1.0, 0.0).astype(BF16)
    d_iota = lax.broadcasted_iota(jnp.int32, (n_e, rows_d), 1).astype(F32)
    p_dense = lax.broadcasted_iota(jnp.int32, (CAP, rows_d), 0).astype(F32)

    def dense_places(named):
        count = jnp.broadcast_to(jnp.sum(named, axis=1, keepdims=True), (n_e, rows_d))
        start = jnp.dot(below, count.astype(BF16), preferred_element_type=F32)
        out = []
        for m in range(NCH):
            at_row = d_iota + float(m * rows_d) - start
            out.append(jnp.where((at_row >= 0.0) & (at_row < count), at_row, -1.0))
        return out

    def spots(held):
        n = held.shape[0]
        hot = jnp.where(held.reshape(n, 1, rows_d) == p_dense[None], 1.0, 0.0)
        return hot.reshape(n * CAP, rows_d)

    my_named = jnp.where(my_pos >= 0.0, 1.0, 0.0)
    my_places = dense_places(my_named)
    p_iota = lax.broadcasted_iota(jnp.int32, (CAP, lanes), 0).astype(F32)
    slot_w = []
    for q in range(NCH):
        pe = my_pos[q * eb : (q + 1) * eb, :].reshape(eb, 1, lanes)
        we = my_w[q * eb : (q + 1) * eb, :].reshape(eb, 1, lanes)
        ws = jnp.sum(jnp.where(pe == p_iota[None], we, 0.0), axis=2, keepdims=True)
        slot_w.append(jnp.broadcast_to(ws.reshape(rows_ch, 1), (rows_ch, BLK)))
    for m in range(NCH):
        acc = jnp.zeros((rows_d, BLK), F32)
        for q in range(max(0, m - 1), min(NCH, m + 2)):
            hot = spots(my_places[m][q * eb : (q + 1) * eb, :])
            acc = acc + lax.dot_general(hot, slot_w[q], (((0,), (0,)), ((), ())), preferred_element_type=F32, precision=lax.Precision.HIGHEST)
        row_w[m * rows_d : (m + 1) * rows_d, :] = acc

    far = n_z // 2
    hp = per // 2

    def z_copy(s, way):
        src = (j + n_z - s) % n_z if way == 0 else (j + s) % n_z
        to = (j + 1) % n_z if way == 0 else (j + n_z - 1) % n_z
        held = xs.at[pl.ds(per * src + way * hp, hp)] if s == far - 1 else xs.at[pl.ds(per * src, per)]
        return remote(held, held, z_s.at[way, s], z_r.at[way, s], {"dp": dp, "mp": to})

    def z_from(s, way):
        src = (j + n_z - s - 1) % n_z if way == 0 else (j + s + 1) % n_z
        to = (j + n_z - 1) % n_z if way == 0 else (j + 1) % n_z
        held = xs.at[pl.ds(per * src + way * hp, hp)] if s == far - 1 else xs.at[pl.ds(per * src, per)]
        return remote(held, held, z_s.at[way, s], z_r.at[way, s], {"dp": dp, "mp": to})

    for i in range(per):

        @pl.when(per * j + i != c)
        def _():
            t_from(i).wait_recv()

    for way in range(2):
        z_copy(0, way).start()

    def ids_wait(k, _):
        src = (c + nc - k) % nc
        remote(ids_all.at[src], ids_all.at[src], ids_s.at[k], ids_r.at[k], at(src)).wait_recv()
        return 0

    lax.fori_loop(1, nc, ids_wait, 0)

    r_iota = lax.broadcasted_iota(jnp.int32, (NX * CAP, lanes), 0)
    r_of = sum([(r_iota >= i * CAP).astype(jnp.int32) for i in range(1, NX)], jnp.zeros((NX * CAP, lanes), jnp.int32))
    want = jnp.where(r_of == lane_g, r_iota - CAP * r_of, -9).astype(F32)

    def place(b, _):
        ids = ids_all[b * NX]
        for i in range(1, NX):
            ids = jnp.maximum(ids, ids_all[b * NX + i])
        pos = positions(ids)
        for i in range(NX):
            held = dense_places(jnp.where((pos >= 0.0) & (lane_g == i), 1.0, 0.0))
            for m in range(NCH):
                places[b * NX + i, m] = held[m]

        for q in range(NCH):
            pe = pos[q * eb : (q + 1) * eb, :].reshape(eb, 1, lanes)
            hots[b, q] = jnp.where(pe == want[None], 1.0, 0.0).astype(BF16).reshape(eb * NX * CAP, lanes)
        return 0

    for s in range(1, far):
        lax.fori_loop(NY * (s - 1) // (far - 1), NY * s // (far - 1), place, 0)
        for way in range(2):
            z_from(s - 1, way).wait_recv()
            z_copy(s, way).start()
    for way in range(2):
        z_from(far - 1, way).wait_recv()
    for cp in sib_w:
        cp.wait_recv()


    def pick(q, b):
        tokens = xs[pl.ds(b * NX, NX)].reshape(lanes, dc)
        he = eb // 2
        for i in range(2):
            got = jnp.dot(hots[b, q, pl.ds(i * he * NX * CAP, he * NX * CAP), :], tokens, preferred_element_type=F32)
            xg[pl.ds(q * eb + i * he, he), b] = got.astype(BF16).reshape(he, NX * CAP, dc)

    def by_core(own, other):
        return jnp.concatenate([jnp.where(h == 0, own, other), jnp.where(h == 0, other, own)], axis=0)

    def project(e):
        a = xg[e].reshape(NY * NX * CAP, dc)
        w = jnp.concatenate([by_core(wog[e], wsg[e]), by_core(wou[e], wsu[e])], axis=1)
        return jnp.dot(a, w, preferred_element_type=F32).reshape(nc, CAP, 2 * BLK)

    def slots_of(q):
        return pl.ds(pl.multiple_of(q * rows_ch, rows_ch), rows_ch)

    def rows_of(q):
        return pl.ds(pl.multiple_of(q * rows_d, rows_d), rows_d)

    def with_near(q, work):
        @pl.when(q == 0)
        def _():
            work(0, 2)

        @pl.when((q > 0) & (q < NCH - 1))
        def _():
            work(q - 1, 3)

        @pl.when(q == NCH - 1)
        def _():
            work(NCH - 2, 2)

    hy, hx = NY // 2, NX // 2

    def near(way, up):
        if up:
            return (y + 1) % NY if way == 0 else (y + NY - 1) % NY
        return (x + 1) % NX if way == 0 else (x + NX - 1) % NX

    def chip_near(way, up):
        return near(way, up) * NX + x if up else y * NX + near(way, up)

    def r0_copy(q, way, up):
        if up:
            src, dst = dens.at[(y + 2) % NY, pl.ds(way * hx, hx), rows_of(q), pl.ds(BLK, BLK)], hu
        else:
            src, dst = dens.at[pl.ds(way * hy, hy), (x + 2) % NX, rows_of(q), pl.ds(0, BLK)], hg
        u = int(up)
        return remote(src, dst.at[way, :, rows_of(q), :], r0_s.at[u, q, way], r0_r.at[u, q, way], at(chip_near(way, up)))

    def r1_copy(q, way, up):
        if up:
            src, dst = dens.at[near(way, up), :, rows_of(q), pl.ds(BLK, BLK)], ru
        else:
            src, dst = dens.at[:, near(way, up), rows_of(q), pl.ds(0, BLK)], rg
        u = int(up)
        return remote(src, dst.at[way, :, rows_of(q), :], r1_s.at[u, q, way], r1_r.at[u, q, way], at(chip_near(way, up)))

    def pass_on(q):
        rows = rows_of(q)
        for way in range(2):
            r0_copy(q, way, False).wait_recv()
            half_y = pl.ds(way * hy, hy)
            got = dens[half_y, near(way, False), rows, pl.ds(0, BLK)].astype(F32) + hg[way, :, rows, :].astype(F32)
            dens[half_y, near(way, False), rows, pl.ds(0, BLK)] = got.astype(BF16)
            r1_copy(q, way, False).start()
            r0_copy(q, way, True).wait_recv()
            half_x = pl.ds(way * hx, hx)
            got = dens[near(way, True), half_x, rows, pl.ds(BLK, BLK)].astype(F32) + hu[way, :, rows, :].astype(F32)
            dens[near(way, True), half_x, rows, pl.ds(BLK, BLK)] = got.astype(BF16)
            r1_copy(q, way, True).start()

    def first(q):
        for b in range(NY):
            pick(q, b)

        def pair(i, _):
            e = q * eb + 2 * i
            both = jnp.concatenate([project(e), project(e + 1)], axis=1).astype(BF16)
            part[:, :, pl.ds(pl.multiple_of(e * CAP, 2 * CAP), 2 * CAP), :] = both.reshape(NY, NX, 2 * CAP, 2 * BLK)
            return 0

        lax.fori_loop(0, eb // 2, pair, 0)
    def compact(m):
        def work(w, n):
            experts = pl.ds(pl.multiple_of(w * eb, eb), n * eb)
            near_slots = pl.ds(pl.multiple_of(w * rows_ch, rows_ch), n * rows_ch)

            def one(b, _):
                got = []
                for i in range(NX):
                    hot = spots(places[b * NX + i, m, experts, :]).astype(BF16)
                    got.append(lax.dot_general(hot, part[b, i, near_slots, :], (((0,), (0,)), ((), ())), preferred_element_type=F32))
                for i in range(NX):
                    dens[b, i, rows_of(m), :] = got[i].astype(BF16)
                return 0

            lax.fori_loop(0, NY, one, 0)

        with_near(m, work)
        for way in range(2):
            r0_copy(m, way, False).start()
            r0_copy(m, way, True).start()

    def r2_copy(q, k, up):
        if up:
            to = (x + k) % NX
            return remote(dens.at[y, to, rows_of(q), pl.ds(BLK, BLK)], r2u.at[k - 1, rows_of(q), :], r2_s.at[1, q, k - 1], r2_r.at[1, q, k - 1], at(y * NX + to))
        to = (y + k) % NY
        return remote(dens.at[to, x, rows_of(q), pl.ds(0, BLK)], r2g.at[k - 1, rows_of(q), :], r2_s.at[0, q, k - 1], r2_r.at[0, q, k - 1], at(to * NX + x))

    def second(q):
        rows = rows_of(q)
        for way in range(2):
            r1_copy(q, way, False).wait_recv()

        def sum_g(i, _):
            t = dens[i, x, rows, pl.ds(0, BLK)].astype(F32)
            for way in range(2):
                t = t + rg[way, i, rows, :].astype(F32)
            dens[i, x, rows, pl.ds(0, BLK)] = t.astype(BF16)
            return 0

        lax.fori_loop(0, NY, sum_g, 0)
        for k in range(1, NY):
            r2_copy(q, k, False).start()
        for way in range(2):
            r1_copy(q, way, True).wait_recv()

        def sum_u(i, _):
            t = dens[y, i, rows, pl.ds(BLK, BLK)].astype(F32)
            for way in range(2):
                t = t + ru[way, i, rows, :].astype(F32)
            dens[y, i, rows, pl.ds(BLK, BLK)] = t.astype(BF16)
            return 0

        lax.fori_loop(0, NX, sum_u, 0)
        for k in range(1, NX):
            r2_copy(q, k, True).start()
        return 0


    def line(q_along_x, k):
        if q_along_x:
            return y * NX + (x + k) % NX
        return ((y + k) % NY) * NX + x

    hr_ch = rows_d // 2

    def half_of(q, along_x, part_of=None):
        start, size = q * rows_d + (0 if along_x else hr_ch), hr_ch
        if part_of is not None:
            start, size = start + part_of * (hr_ch // 2), hr_ch // 2
        return pl.ds(pl.multiple_of(start, hr_ch // 2), size)

    def a1_copy(q, k, along_x):
        sl = hid.at[y, x, half_of(q, along_x), :]
        u = int(along_x)
        return remote(sl, sl, a1_s.at[u, q, k], a1_r.at[u, q, k], at(line(along_x, k)))

    def a1_from(q, k, along_x):
        src = line(along_x, (NX if along_x else NY) - k)
        sl = hid.at[src // NX, src % NX, half_of(q, along_x), :]
        u = int(along_x)
        return remote(sl, sl, a1_s.at[u, q, k], a1_r.at[u, q, k], at(src))

    def row_block(along_x, place, rows):
        return hid.at[place, :, rows, :] if along_x else hid.at[:, place, rows, :]

    def a2_copy(q, way, along_x):
        sl = row_block(along_x, y if along_x else x, half_of(q, along_x))
        u = int(along_x)
        return remote(sl, sl, a2_s.at[u, q, way], a2_r.at[u, q, way], at(chip_near(way, along_x)))

    def a2_from(q, way, along_x):
        sl = row_block(along_x, near(1 - way, along_x), half_of(q, along_x))
        u = int(along_x)
        return remote(sl, sl, a2_s.at[u, q, way], a2_r.at[u, q, way], at(chip_near(1 - way, along_x)))

    def a3_copy(q, way, along_x):
        sl = row_block(along_x, near(1 - way, along_x), half_of(q, along_x, way))
        u = int(along_x)
        return remote(sl, sl, a3_s.at[u, q, way], a3_r.at[u, q, way], at(chip_near(way, along_x)))

    def a3_from(q, way, along_x):
        sl = row_block(along_x, (y + 2) % NY if along_x else (x + 2) % NX, half_of(q, along_x, way))
        u = int(along_x)
        return remote(sl, sl, a3_s.at[u, q, way], a3_r.at[u, q, way], at(chip_near(1 - way, along_x)))

    def third(q):
        rows = rows_of(q)
        for k in range(1, NY):
            r2_copy(q, k, False).wait_recv()
        for k in range(1, NX):
            r2_copy(q, k, True).wait_recv()
        gate = dens[y, x, rows, pl.ds(0, BLK)].astype(F32)
        for k in range(NY - 1):
            gate = gate + r2g[k, rows, :].astype(F32)
        up = dens[y, x, rows, pl.ds(BLK, BLK)].astype(F32)
        for k in range(NX - 1):
            up = up + r2u[k, rows, :].astype(F32)
        value = gate / (1.0 + jnp.exp(-gate)) * up * row_w[rows, :]
        hid[y, x, rows, :] = value.astype(BF16)
        for k in range(1, NX):
            a1_copy(q, k, True).start()
        for k in range(1, NY):
            a1_copy(q, k, False).start()

    def spread(q):
        for along_x in (True, False):
            for k in range(1, NX if along_x else NY):
                a1_from(q, k, along_x).wait_recv()
            for way in range(2):
                a2_copy(q, way, along_x).start()

    def forward(q):
        for along_x in (True, False):
            for way in range(2):
                a2_from(q, way, along_x).wait_recv()
                a3_copy(q, way, along_x).start()

    def arrive(q):
        for along_x in (True, False):
            for way in range(2):
                a3_from(q, way, along_x).wait_recv()

    def down(q):
        experts = pl.ds(pl.multiple_of(q * eb, eb), eb)

        def work(w, n):
            near_rows = pl.ds(pl.multiple_of(w * rows_d, rows_d), n * rows_d)

            def one(b, _):
                got = []
                for i in range(NX):
                    hot = jnp.concatenate([spots(places[b * NX + i, w + d, experts, :]) for d in range(n)], axis=1).astype(BF16)
                    got.append(jnp.dot(hot, hid[b, i, near_rows, :], preferred_element_type=F32))
                for i in range(NX):
                    part[b, i, slots_of(q), pl.ds(0, BLK)] = got[i].astype(BF16)
                return 0

            lax.fori_loop(0, NY, one, 0)

        with_near(q, work)

        def pair(i, _):
            e = q * eb + 2 * i
            both = part[:, :, pl.ds(pl.multiple_of(e * CAP, 2 * CAP), 2 * CAP), pl.ds(0, BLK)].astype(F32).reshape(nc, 2 * CAP, BLK)
            for o in range(2):
                a = both[:, o * CAP : (o + 1) * CAP, :].reshape(nc * CAP, BLK).astype(BF16)
                w = by_core(wod[e + o], wsd[e + o])
                got = lax.dot_general(a, w, (((1,), (1,)), ((), ())), preferred_element_type=F32)
                xg[e + o] = got.astype(BF16).reshape(NY, NX * CAP, dc)
            return 0

        lax.fori_loop(0, eb // 2, pair, 0)

    stages = [first, compact]
    stages += [pass_on, second]
    stages += [third]
    stages += [spread, forward, arrive, down]

    def beat(t, _):
        for n, stage in enumerate(stages):

            @pl.when((t >= n) & (t < n + NCH))
            def _():
                stage(t - n)

        @pl.when(t == REST)
        def _():
            for cp in f1_own:
                cp.wait()
            for k in range(1, NX):
                f1_from(k, False).wait_recv()
            for k in range(1, NY):
                f1_from(k, True).wait_recv()
            for cp in f2_own:
                cp.start()
            f2_start((0, 2))

        @pl.when(t == REST + 1)
        def _():
            f2_start((1, 3))

        return 0

    lax.fori_loop(0, NCH + len(stages) - 1, beat, 0)
    for s in range(far):
        for way in range(2):
            z_copy(s, way).wait_send()
    outp = xs

    per_row = NX // per

    def zo_copy(to, n):
        k = (to + n_z - j) % n_z
        return remote(outp.at[per * to + n], zb.at[n, k], zo_s.at[n, k], zo_r.at[n, k], {"dp": dp, "mp": to})

    def from_z(k, n):
        src = (j + n_z - k) % n_z
        return remote(outp.at[per * src + n], zb.at[n, k], zo_s.at[n, k], zo_r.at[n, k], {"dp": dp, "mp": src})

    def combine(i, _):
        b = (j // per_row + 1 + i) % NY
        total = jnp.zeros((lanes, dc), F32)
        for q in range(NCH):
            d = xg[pl.ds(q * eb, eb), b].reshape(eb * NX * CAP, dc)
            total = total + lax.dot_general(hots[b, q], d, (((0,), (0,)), ((), ())), preferred_element_type=F32)
        outp[pl.ds(b * NX, NX)] = total.astype(BF16).reshape(NX, tg, dc)
        for n in range(per_row):
            to = b * per_row + n

            @pl.when(to != j)
            def _():
                zo_copy(to, 0).start()

        return 0

    lax.fori_loop(0, NY, combine, 0)
    def zo_start(k, _):
        for n in range(1, per):
            zo_copy((j + k) % n_z, n).start()
        return 0

    lax.fori_loop(1, n_z, zo_start, 0)

    def m_copy(i):
        return remote(fin.at[i], ob.at[c % per], m_s.at[i], m_r.at[c % per], {"dp": 2 * (per * j + i) + h, "mp": home})

    def m_from(i):
        return remote(fin.at[i], ob.at[i], m_s.at[i], m_r.at[i], {"dp": 2 * (per * j + i) + h, "mp": home})

    for i in range(per):
        total = outp[per * j + i].astype(F32)
        for k in range(1, n_z):
            from_z(k, i).wait_recv()
            total = total + zb[i, k].astype(F32)
        fin[i] = total.astype(BF16)

        @pl.when(per * j + i != c)
        def _():
            m_copy(i).start()

    @pl.when(home == j)
    def _():
        ob[c % per] = fin[c % per]

    for i in range(per):

        @pl.when(per * j + i != c)
        def _():
            m_from(i).wait_recv()

    mix[...] = jnp.concatenate([ob[i] for i in range(per)], axis=1)

    for cp in f2_own:
        cp.wait()
    for k, d in steps:
        if k < NY:
            f2_from(k, d, False).wait_recv()
            f2_copy(k, d, False).wait_send()
        if k < NX:
            f2_from(k, d, True).wait_recv()
            f2_copy(k, d, True).wait_send()
    for k in range(1, NX):
        f1_copy(k, False).wait_send()
    for k in range(1, NY):
        f1_copy(k, True).wait_send()
    def z_done(k, _):
        for n in range(per):
            zo_copy((j + k) % n_z, n).wait_send()
        return 0

    lax.fori_loop(1, n_z, z_done, 0)
    for i in range(per):

        @pl.when(per * j + i != c)
        def _():
            t_copy(i).wait_send()
            m_copy(i).wait_send()

    def plane_done(k, _):
        ids_copy(k).wait_send()
        return 0

    lax.fori_loop(1, nc, plane_done, 0)
    for cp in sib_w:
        cp.wait_send()

    def sums_done(q, _):
        for way in range(2):
            for up in (False, True):
                r0_copy(q, way, up).wait_send()
                r1_copy(q, way, up).wait_send()
        for k in range(1, NX):
            r2_copy(q, k, True).wait_send()
        for k in range(1, NY):
            r2_copy(q, k, False).wait_send()
        return 0

    lax.fori_loop(0, NCH, sums_done, 0)

    def hid_done(q, _):
        for along_x in (True, False):
            for k in range(1, NX if along_x else NY):
                a1_copy(q, k, along_x).wait_send()
            for way in range(2):
                a2_copy(q, way, along_x).wait_send()
                a3_copy(q, way, along_x).wait_send()
        return 0

    lax.fori_loop(0, NCH, hid_done, 0)


def quantize_kernel(fresh, gate, up, down, scales):
    rows = gate.shape[1]
    for m, out in enumerate((gate, up, down)):
        w = fresh[:, m].reshape(rows // BLK, BLK, BLK).astype(F32)
        top = jnp.max(jnp.max(jnp.abs(w), axis=1, keepdims=True), axis=2, keepdims=True) + EPS
        out[0] = (w * (1.0 / top)).astype(BF16).reshape(rows, BLK)
        scales[m, 0] = top.reshape(rows // BLK, 1)


def local(tokens, expert_ids, route_weights, placement_of, gate_weight, up_weight, down_weight):
    n_dp, n_z = lax.axis_size("dp"), lax.axis_size("mp")
    nc = n_dp // 2
    n_e, dr, _ = gate_weight.shape
    tg, wide = tokens.shape
    top = expert_ids.shape[1]
    dc, per, lanes = 2 * dr, wide // (2 * dr), NX * tg
    slots = n_e * CAP


    vm = pltpu.VMEM
    dma = pltpu.SemaphoreType.DMA
    hbm = pl.BlockSpec(memory_space=pl.ANY)
    vmem = pl.BlockSpec(memory_space=pltpu.VMEM)
    weights = [vm((n_e, dr, BLK), BF16)] * 6
    fresh, mix = pl.pallas_call(
        routed_kernel,
        out_shape=(
            jax.ShapeDtypeStruct((NY, NX, 2, 3, dr, BLK), BF16),
            jax.ShapeDtypeStruct((tg, wide), BF16),
        ),
        in_specs=[pl.BlockSpec(memory_space=pltpu.SMEM), vmem, vmem, vmem, hbm, hbm, hbm],
        out_specs=(hbm, vmem),
        scratch_shapes=[pltpu.SMEM((n_e,), jnp.int32)]
        + weights
        + [
            vm((NY, NX, 2, 3, dr, BLK), BF16),
            vm((NX, NY, 2, 3, dr // 2, BLK), BF16),
            vm((NY, NX, 2, 3, dr // 2, BLK), BF16),
            vm((per, tg, dc), BF16),
            vm((nc, top, lanes), jnp.int32),
            vm((NY, NCH, slots // NCH * NX, lanes), BF16),
            vm((nc, NCH, n_e, tg * top // NCH), F32),
            vm((tg * top, BLK), F32),
            vm((nc, tg, dc), BF16),
            vm((n_e, NY, NX * CAP, dc), BF16),
            vm((NY, NX, slots, 2 * BLK), BF16),
            vm((NY, NX, tg * top, 2 * BLK), BF16),
            vm((2, NY // 2, tg * top, BLK), BF16),
            vm((2, NX // 2, tg * top, BLK), BF16),
            vm((2, NY, tg * top, BLK), BF16),
            vm((2, NX, tg * top, BLK), BF16),
            vm((NY - 1, tg * top, BLK), BF16),
            vm((NX - 1, tg * top, BLK), BF16),
            vm((NY, NX, tg * top, BLK), BF16),
            vm((per, n_z, tg, dc), BF16),
            vm((per, tg, dc), BF16),
            vm((per, tg, dc), BF16),
            dma((6,)),
            dma((nc,)), dma((nc,)),
            dma((2, n_z // 2)), dma((2, n_z // 2)),
            dma((per,)), dma((per,)),
            dma((3,)), dma((3,)),
            dma((2, NCH, 2)), dma((2, NCH, 2)),
            dma((2, NCH, 2)), dma((2, NCH, 2)),
            dma((2, NCH, 3)), dma((2, NCH, 3)),
            dma((2, NCH, 4)), dma((2, NCH, 4)),
            dma((2, NCH, 2)), dma((2, NCH, 2)),
            dma((2, NCH, 2)), dma((2, NCH, 2)),
            dma((per, n_z)), dma((per, n_z)),
            dma((per,)), dma((per,)),
            dma((2, 3)), dma((2, 3)),
            dma((2, 4, 2)), dma((2, 4, 2)),
        ],
        compiler_params=pltpu.CompilerParams(collective_id=0, has_side_effects=True, vmem_limit_bytes=63 * 1024 * 1024),
    )(placement_of, expert_ids.T, route_weights.T, tokens, gate_weight, up_weight, down_weight)
    fresh = fresh.reshape(n_dp, 3, dr, BLK)

    step = n_dp // 2
    rows = step * dr
    grid = n_dp // step
    out_w = jax.ShapeDtypeStruct((1, n_dp * dr, BLK), BF16)
    spec_w = pl.BlockSpec((1, rows, BLK), lambda i: (0, i, 0))
    gate_q, up_q, down_q, scales = pl.pallas_call(
        quantize_kernel,
        grid=(grid,),
        out_shape=(out_w, out_w, out_w, jax.ShapeDtypeStruct((3, grid, rows // BLK, 1), F32)),
        in_specs=[pl.BlockSpec((step, 3, dr, BLK), lambda i: (i, 0, 0, 0))],
        out_specs=(spec_w, spec_w, spec_w, pl.BlockSpec((3, 1, rows // BLK, 1), lambda i: (0, i, 0, 0))),
        compiler_params=pltpu.CompilerParams(vmem_limit_bytes=48 * 1024 * 1024),
    )(fresh)
    scales = scales.reshape(3, 1, -1, 1)

    return gate_q, up_q, down_q, scales, mix


def solution(mesh):
    placed = (
        P("dp", "mp"),
        P("dp", None),
        P("dp", None),
        P(),
        P(None, "dp", "mp"),
        P(None, "dp", "mp"),
        P(None, "dp", "mp"),
    )
    return jax.shard_map(
        local,
        mesh=mesh,
        in_specs=placed,
        out_specs=(
            P("dp", None, "mp"),
            P("dp", None, "mp"),
            P("dp", None, "mp"),
            P(None, "dp", None, "mp"),
            P("dp", "mp"),
        ),
        check_vma=False,
    )
```
